32 devices in a mesh: groups: 2 (over y), query: 2 (over x), car: 4 (over z), replica: 2 (over core).
Axes of the slice: x: 2, y: 2, z: 4, core: 2. Of those that a mesh axis runs over, the one named last changes fastest.
Arguments:
- query_heads: bfloat16 [16384, 768], P(('groups', 'query', 'car', 'replica')), parts along dimension 0, may hold values from -140 to 140
- d_out: bfloat16 [16384, 768], P(('groups', 'query', 'car', 'replica')), parts along dimension 0, may hold values from -0.375 to 0.375
- anchor_kv: bfloat16 [8, 8, 1536], P(('groups', 'car'), 'query'), parts along dimension 0, may hold values from -8 to 8
- point_counts: int32 [32, 4], P(('groups', 'query', 'car', 'replica')), parts along dimension 0, may hold values from 1 to 256, 512 in all within a row
- slot_car: int32 [8], P('groups'), parts along dimension 0, may hold values from 0 to 3, each once
- out_weight: bfloat16 [768, 768], replicated, may hold values from -1.75 to 1.75
Outputs:
- grad_queries: bfloat16 [16384, 768], P(('groups', 'query', 'car', 'replica')), parts along dimension 0
- grad_kv: float32 [8, 8, 1536], P(('groups', 'car'), 'query'), parts along dimension 0
- grad_out_weight: float32 [1536, 768], P('groups'), parts along dimension 0
The draws below stay inside these ranges and needn't reach their ends.
There are 2 independent parts, one for each index of `groups`. The reference program is written for one: setup_inputs(seed, part) draws one part's arguments, and reference() takes and returns one part's arrays. A program takes and returns all parts, laid end to end along the dimension named above; an argument that names none is the same for every part. Nothing has to cross between parts.
Inputs may be any that keep to these rules, and one draw needn't show every extreme that they name: `point_counts`: in every shard some car has exactly 256 points. `slot_car`: each car stands in exactly one slot.
All inputs are finite; a program needn't handle non-finite values.
Results may differ from the reference program's by a relative error of at most 0.013.
Values may be sent and summed in bfloat16 or wider, within the bound.
A program may use at most 64 MiB of HBM per device.

```python
import math
import jax
import jax.numpy as jnp
import numpy as np
from jax import lax

D = 768
HEADS = 12
HEAD_DIM = 64
Q_DEV = 512
CARS = 4
ANCH = 8
SHARDS = 16
POINTS = 8192


def draw_query_heads(key, part):
    key = jax.random.fold_in(key, 1)
    values = jax.random.normal(key, (POINTS, D), jnp.float32)
    return jnp.clip(values, -140.0, 140.0).astype(jnp.bfloat16)


def draw_anchor_kv(key, part):
    key = jax.random.fold_in(key, 2)
    values = jax.random.normal(key, (CARS, ANCH, 2 * D), jnp.float32)
    return jnp.clip(values, -8.0, 8.0).astype(jnp.bfloat16)


def steps_of(rng, shape, pieces, least, largest):
    level, own = 1.0, jax.random.fold_in(rng, 6)
    for position, shards_of in pieces:
        heights = jnp.exp(jax.random.uniform(jax.random.fold_in(own, position), (shards_of,), jnp.float32, least / len(pieces), largest / len(pieces)))
        level = level * jnp.repeat(heights, shape[position] // shards_of).reshape([-1 if axis == position else 1 for axis in range(len(shape))])
    return level


def length_profile(number_of, total, bound, lean):
    weights = [(1 << 20) // math.isqrt(rank ** lean) + 1 for rank in range(2, number_of + 1)]
    surplus, given = total - bound - (number_of - 1), [1] * (number_of - 1)
    while surplus > 0:
        free = [i for i in range(number_of - 1) if given[i] < bound]
        pool, left = sum([weights[i] for i in free]), surplus
        for i in free:
            extra = min(bound - given[i], max(1, left * weights[i] // pool), surplus)
            given[i] = given[i] + extra
            surplus = surplus - extra
    return np.array([bound] + given)


def ragged(key, amount, total, most, skew):
    if amount == 2:
        one = jax.random.randint(key, (), max(1, total - most), min(most, total - 1) + 1)
        return jnp.stack([one, total - one])
    lengths = jnp.asarray(length_profile(amount, total, most, skew), jnp.int32)
    twos = (amount - 1) // 2
    donor, receiver = lengths[1:1 + 2 * twos:2], lengths[2:2 + 2 * twos:2]
    margin = jnp.minimum(donor - 1, most - receiver)
    moved = jax.random.randint(jax.random.fold_in(key, 1), (twos,), 0, 1 << 20) % (margin + 1)
    lengths = lengths.at[1:1 + 2 * twos:2].set(donor - moved).at[2:2 + 2 * twos:2].set(receiver + moved)
    return lengths[jax.random.permutation(jax.random.fold_in(key, 2), amount)]


def noise(key, extent, deviation, bound, shards=(), kind=jnp.bfloat16):
    drawn = jax.random.normal(key, extent, jnp.float32) * deviation
    if len(shards) > 0:
        drawn = steps_of(key, extent, shards, -0.22, 0.18) * drawn
    return jnp.clip(drawn, min=-bound, max=bound).astype(kind)


def setup_inputs(seed: int = 0, part: int = 0) -> dict:
    key_list = jax.random.split(jax.random.key(seed), 7)
    part_splits = jax.random.split(jax.random.fold_in(key_list[6], part), 7)
    return {
        "query_heads": draw_query_heads(jax.random.fold_in(jax.random.fold_in(key_list[6], part), 71), part),
        "d_out": noise(part_splits[1], (POINTS, D), 0.0625, 0.375, ((0, 16),)),
        "anchor_kv": draw_anchor_kv(jax.random.fold_in(jax.random.fold_in(key_list[6], part), 71), part),
        "point_counts": jax.vmap(lambda own: ragged(own, CARS, Q_DEV, Q_DEV // 2, 2))(jax.random.split(part_splits[3], SHARDS)).reshape((SHARDS, CARS)).astype(jnp.int32),
        "slot_car": jax.random.permutation(part_splits[4], CARS).astype(jnp.int32),
        "out_weight": noise(key_list[5], (D, D), (D // 64) ** -0.5, 1.75),
    }


def rounded(values):
    return lax.optimization_barrier(values.astype(jnp.bfloat16)).astype(jnp.float32)


def reference(query_heads, d_out, anchor_kv, point_counts, slot_car, out_weight):
    scale = HEAD_DIM ** -0.5
    keys_total = CARS * ANCH
    ends = jnp.cumsum(point_counts, axis=1)
    local = jnp.arange(Q_DEV, dtype=jnp.int32)
    point_car = jnp.sum((local[None, :, None] >= ends[:, None, :]).astype(jnp.int32), axis=2)
    flat_kv = anchor_kv.reshape(keys_total, 2 * D)
    key_car = jnp.repeat(slot_car, ANCH)
    keys = flat_kv[:, :D].reshape(keys_total, HEADS, HEAD_DIM).astype(jnp.float32)
    values = flat_kv[:, D:].reshape(keys_total, HEADS, HEAD_DIM).astype(jnp.float32)
    queries = query_heads.reshape(SHARDS, Q_DEV, D)
    cotangents = d_out.reshape(SHARDS, Q_DEV, D)

    def block(carry, inputs):
        weight_sum, kv_sum = carry
        query_block, grad_block, car_block = inputs
        q_heads = query_block.reshape(Q_DEV, HEADS, HEAD_DIM).astype(jnp.float32)
        scores = jnp.einsum('qhe,khe->qhk', q_heads, keys) * scale
        allowed = (car_block[:, None] == key_car[None, :])[:, None, :]
        best = jnp.max(jnp.where(allowed, scores, -1e30), axis=2)
        weights = jnp.where(allowed, jnp.exp(scores - best[:, :, None]), 0.0)
        total = jnp.sum(weights, axis=2)
        accum = jnp.einsum('qhk,khe->qhe', rounded(weights), values)
        attended = (accum / total[:, :, None]).reshape(Q_DEV, D).astype(jnp.bfloat16)
        d_att = jnp.dot(grad_block, out_weight.T, preferred_element_type=jnp.float32).astype(jnp.bfloat16)
        weight_sum = weight_sum + jnp.dot(attended.T, grad_block, preferred_element_type=jnp.float32)
        d_heads = d_att.reshape(Q_DEV, HEADS, HEAD_DIM).astype(jnp.float32)
        delta = jnp.sum(d_heads * attended.reshape(Q_DEV, HEADS, HEAD_DIM).astype(jnp.float32), axis=2)
        prob = weights / total[:, :, None]
        d_prob = jnp.einsum('qhe,khe->qhk', d_heads, values)
        d_score = rounded(prob * (d_prob - delta[:, :, None]))
        d_query = (jnp.einsum('qhk,khe->qhe', d_score, keys) * scale).reshape(Q_DEV, D).astype(jnp.bfloat16)
        d_key = jnp.einsum('qhk,qhe->khe', d_score, q_heads) * scale
        d_value = jnp.einsum('qhk,qhe->khe', rounded(prob), d_heads)
        kv_sum = kv_sum + jnp.concatenate([d_key.reshape(keys_total, D), d_value.reshape(keys_total, D)], axis=1)
        return (weight_sum, kv_sum), d_query

    start = (jnp.zeros((D, D), jnp.float32), jnp.zeros((keys_total, 2 * D), jnp.float32))
    (weight_sum, kv_sum), d_queries = lax.scan(block, start, (queries, cotangents, point_car))
    return d_queries.reshape(POINTS, D), kv_sum.reshape(CARS, ANCH, 2 * D), weight_sum
```

```python
import functools
import math

import jax
import jax.numpy as jnp
from jax import lax
from jax.experimental import pallas as pl
from jax.experimental.pallas import tpu as pltpu
from jax.sharding import PartitionSpec as P

D = 768
HEADS = 12
HEAD_DIM = 64


def head_view(values):
    return values.reshape(values.shape[0], HEADS, HEAD_DIM)


def car_lookup(start, count, anchors_each, owners, slot_car):
    rows = start + jnp.arange(count, dtype=jnp.int32)
    slots = rows // anchors_each % owners
    table = slots[:, None] == jnp.arange(slot_car.shape[0], dtype=jnp.int32)[None, :]
    return jnp.sum(jnp.where(table, slot_car[None, :], 0), axis=1)


def body(query_heads, d_out, anchor_kv, point_counts, slot_car, out_weight):
    scale = HEAD_DIM ** (-0.5)
    owners = lax.axis_size("car")
    anchors_each = anchor_kv.shape[1]
    rows_here = query_heads.shape[0]
    ends = jnp.cumsum(point_counts[0])
    local = jnp.arange(rows_here, dtype=jnp.int32)
    point_car = jnp.sum((local[:, None] >= ends[None, :]).astype(jnp.int32), axis=1)
    panel = anchor_kv[0]
    queries = head_view(query_heads)

    def allowed_for(start, count):
        cars = car_lookup(start, count, anchors_each, owners, slot_car)
        return (point_car[:, None] == cars[None, :])[:, None, :]

    def forward_step(carry, piece, start):
        best, total, accum = carry
        count = piece.shape[0]
        keys = head_view(piece[:, :D])
        values = head_view(piece[:, D:])
        allowed = allowed_for(start, count)
        scores = (
            jnp.einsum("qhe,khe->qhk", queries, keys, preferred_element_type=jnp.float32) * scale
        )
        peak = jnp.max(jnp.where(allowed, scores, -1e30), axis=2)
        new_best = jnp.maximum(best, peak)
        weights = jnp.where(allowed, jnp.exp(scores - new_best[:, :, None]), 0.0)
        fade = jnp.exp(best - new_best)
        total = total * fade + jnp.sum(weights, axis=2)
        accum = accum * fade[:, :, None] + jnp.einsum(
            "qhk,khe->qhe", weights.astype(jnp.bfloat16), values, preferred_element_type=jnp.float32
        )
        return (new_best, total, accum)

    init = (
        jnp.full((rows_here, HEADS), -1e30, jnp.float32),
        jnp.zeros((rows_here, HEADS), jnp.float32),
        jnp.zeros((rows_here, HEADS, HEAD_DIM), jnp.float32),
    )
    kv_all = lax.all_gather(panel, ("query", "car"), axis=0, tiled=True)
    key_rows = kv_all.shape[0]
    block = math.gcd(key_rows, 128)
    blocks = kv_all.reshape(key_rows // block, block, 2 * D)

    def scan_forward(carry, inputs):
        piece, number = inputs
        return (forward_step(carry, piece, number * block), None)

    (best, total, accum), _ = lax.scan(
        scan_forward, init, (blocks, jnp.arange(key_rows // block, dtype=jnp.int32))
    )
    numbers = jnp.arange(key_rows // block, dtype=jnp.int32)
    attended = (accum / total[:, :, None]).reshape(rows_here, D).astype(jnp.bfloat16)
    d_att = lax.dot_general(
        d_out, out_weight, (((1,), (1,)), ((), ())), preferred_element_type=jnp.float32
    ).astype(jnp.bfloat16)
    weight_term = lax.dot_general(
        attended, d_out, (((0,), (0,)), ((), ())), preferred_element_type=jnp.float32
    )
    weight_grad = lax.psum(weight_term, ("query", "car", "replica"))
    d_heads = head_view(d_att)
    delta = jnp.sum(d_heads.astype(jnp.float32) * head_view(attended).astype(jnp.float32), axis=2)

    def backward_step(d_query, inputs):
        piece, number = inputs
        keys = head_view(piece[:, :D])
        values = head_view(piece[:, D:])
        allowed = allowed_for(number * block, block)
        scores = (
            jnp.einsum("qhe,khe->qhk", queries, keys, preferred_element_type=jnp.float32) * scale
        )
        prob = jnp.where(allowed, jnp.exp(scores - best[:, :, None]), 0.0) / total[:, :, None]
        d_prob = jnp.einsum("qhe,khe->qhk", d_heads, values, preferred_element_type=jnp.float32)
        d_score = (prob * (d_prob - delta[:, :, None])).astype(jnp.bfloat16)
        d_query = d_query + jnp.einsum(
            "qhk,khe->qhe", d_score, keys, preferred_element_type=jnp.float32
        )
        d_key = (
            jnp.einsum("qhk,qhe->khe", d_score, queries, preferred_element_type=jnp.float32) * scale
        )
        d_value = jnp.einsum(
            "qhk,qhe->khe", prob.astype(jnp.bfloat16), d_heads, preferred_element_type=jnp.float32
        )
        return (
            d_query,
            jnp.concatenate([d_key.reshape(block, D), d_value.reshape(block, D)], axis=1),
        )

    d_query, stacked = lax.scan(
        backward_step, jnp.zeros((rows_here, HEADS, HEAD_DIM), jnp.float32), (blocks, numbers)
    )
    kv_term = stacked.reshape(key_rows, 2 * D)
    kv_part = lax.psum_scatter(kv_term, ("query", "car"), scatter_dimension=0, tiled=True)
    kv_mine = lax.psum(kv_part, "replica")
    grad_queries = (d_query * scale).reshape(rows_here, D).astype(jnp.bfloat16)
    return (grad_queries, kv_mine.reshape(1, anchors_each, 2 * D), weight_grad)


TILE = 128
GROUP = 4
NT = (((1,), (1,)), ((), ()))
TN = (((0,), (0,)), ((), ()))


def dot(a, b, dims=(((1,), (0,)), ((), ()))):
    return lax.dot_general(a, b, dims, preferred_element_type=jnp.float32)


def fused_kernel(
    xs, zs, counts, slots, kv, q_hbm, do_hbm, w_hbm, gq_hbm, gkv, gw_hbm,
    q, do, w, pack, kvall, da, kbd, vbd, prob_s, ds_s, gq_v, gw_v, mb, pair, rs_out, rs_in, ag, dk,
    in_sem, out_sem, kv_send, kv_recv, pair_sem, rs_send, rs_recv, ag_send, ag_recv,
    fw_send, fw_recv, dk_sem,
):
    scale = HEAD_DIM ** (-0.5)
    chips = xs * zs
    groups = HEADS // GROUP
    rows = q.shape[0]
    grp, x, z, core = (lax.axis_index(a) for a in ("groups", "query", "car", "replica"))
    me = x * zs + z
    other = 1 - core
    sibling = (grp, x, z, other)

    def chip(offset):
        n = lax.rem(me + offset, chips)
        return n, (grp, n // zs, lax.rem(n, zs), core)

    def remote(src, dst, send, recv, device):
        return pltpu.make_async_remote_copy(
            src_ref=src, dst_ref=dst, send_sem=send, recv_sem=recv, device_id=device,
            device_id_type=pl.DeviceIdType.MESH,
        )

    loads = [
        pltpu.make_async_copy(a, b, in_sem.at[i])
        for i, (a, b) in enumerate(((do_hbm, do), (w_hbm, w), (q_hbm, q)))
    ]
    for load in loads:
        load.start()

    barrier = pltpu.get_barrier_semaphore()
    for offset in range(1, chips):
        pl.semaphore_signal(
            barrier, inc=1, device_id=chip(offset)[1], device_id_type=pl.DeviceIdType.MESH
        )
    pl.semaphore_signal(barrier, inc=1, device_id=sibling, device_id_type=pl.DeviceIdType.MESH)

    own_kv = kv[0].astype(jnp.float32)
    for h in range(HEADS):
        pack[h * 4 : h * 4 + 4, :HEAD_DIM] = own_kv[:, h * HEAD_DIM : (h + 1) * HEAD_DIM]
        pack[h * 4 : h * 4 + 4, HEAD_DIM:] = own_kv[:, D + h * HEAD_DIM : D + (h + 1) * HEAD_DIM]
    kvall[me] = pack[...].astype(jnp.bfloat16)

    pl.semaphore_wait(barrier, chips)
    kv_out = []
    for offset in range(1, chips):
        n, device = chip(offset)
        copy = remote(
            kvall.at[me], kvall.at[me], kv_send.at[offset - 1], kv_recv.at[offset - 1], device
        )
        copy.start()
        kv_out.append(copy)

    loads[0].wait()
    loads[1].wait()
    for g in range(groups):
        cols = slice(g * 256, g * 256 + 256)
        da[:, cols] = dot(do[...], w[cols, :], NT).astype(jnp.bfloat16)
    loads[2].wait()

    lane = lax.broadcasted_iota(jnp.int32, (8, rows), 1)
    sub = lax.broadcasted_iota(jnp.int32, (8, rows), 0)
    masks = []
    for s in range(zs):
        car = slots[s]
        first = jnp.int32(0)
        size = jnp.int32(0)
        for c in range(counts.shape[1]):
            first = first + jnp.where(c < car, counts[0, c], 0)
            size = size + jnp.where(c == car, counts[0, c], 0)
        masks.append((lane >= first) & (lane < first + size))

    def swap(v, s):
        return jnp.where((sub & s) == 0, pltpu.roll(v, 8 - s, 0), pltpu.roll(v, s, 0))

    def over_four(v, op):
        v = op(v, swap(v, 1))
        return op(v, swap(v, 2))

    def pick(full, xi, hp):
        part = [full[(xi * zs + s) * 16 + hp * 8 : (xi * zs + s) * 16 + hp * 8 + 8, :] for s in range(zs)]
        out = part[0]
        for s in range(1, zs):
            out = jnp.where(masks[s], part[s], out)
        return out

    for offset in range(1, chips):
        n, device = chip(chips - offset)
        remote(
            kvall.at[n], kvall.at[n], kv_send.at[offset - 1], kv_recv.at[offset - 1], device
        ).wait_recv()

    krows = chips * 16
    diag_row = lax.broadcasted_iota(jnp.int32, (krows, 256), 0) // 4 % GROUP
    diag = diag_row == lax.broadcasted_iota(jnp.int32, (krows, 256), 1) // HEAD_DIM
    half = lax.broadcasted_iota(jnp.int32, (krows, TILE), 1) < HEAD_DIM
    key_tiles = []
    for g in range(groups):
        cols = slice(g * 256, g * 256 + 256)
        both = kvall[:, g * 16 : g * 16 + 16, :].reshape(krows, TILE).astype(jnp.float32)
        turned = pltpu.roll(both, HEAD_DIM, 1)
        keys2 = jnp.where(half, both, turned)
        vals2 = jnp.where(half, turned, both)
        kd = jnp.where(diag, jnp.concatenate([keys2, keys2], axis=1), 0.0).astype(jnp.bfloat16)
        vd = jnp.where(diag, jnp.concatenate([vals2, vals2], axis=1), 0.0).astype(jnp.bfloat16)
        kbd[g] = kd
        vbd[g] = vd
        scores = dot(kd, q[:, cols], NT)
        d_prob = dot(vd, da[:, cols], NT)
        probs = [[None, None] for _ in range(xs)]
        dss = [[None, None] for _ in range(xs)]
        for hp in range(2):
            sc = [pick(scores, xi, hp) * scale for xi in range(xs)]
            dp = [pick(d_prob, xi, hp) for xi in range(xs)]
            best = over_four(functools.reduce(jnp.maximum, sc), jnp.maximum)
            wt = [jnp.exp(v - best) for v in sc]
            total = over_four(functools.reduce(jnp.add, wt), jnp.add)
            inv = 1.0 / total
            pr = [v * inv for v in wt]
            delta = over_four(functools.reduce(jnp.add, [a * b for a, b in zip(pr, dp)]), jnp.add)
            for xi in range(xs):
                probs[xi][hp] = pr[xi]
                dss[xi][hp] = pr[xi] * (dp[xi] - delta)
        for xi in range(xs):
            for s in range(zs):
                at = slice((xi * zs + s) * 16, (xi * zs + s) * 16 + 16)
                mask = jnp.concatenate([masks[s], masks[s]], axis=0)
                prob_s[at, :] = jnp.where(mask, jnp.concatenate(probs[xi], axis=0), 0.0).astype(
                    jnp.bfloat16
                )
                ds_s[g, at, :] = jnp.where(mask, jnp.concatenate(dss[xi], axis=0), 0.0).astype(
                    jnp.bfloat16
                )
        term = dot(prob_s[...], do[...]).astype(jnp.bfloat16)
        for c in range(2):
            for t in range(3):
                at = (c * 3 + t) * TILE
                mb[c, :, t * 48 + g * 16 : t * 48 + g * 16 + 16, :] = term[
                    :, at : at + TILE
                ].reshape(chips, 16, TILE)
        d_key = jnp.where(diag, dot(ds_s[g], q[:, cols]), 0.0) * scale
        d_key = d_key.reshape(chips, 2, 8, 256)
        d_key = d_key[:, 0] + d_key[:, 1]
        d_key = d_key + pltpu.roll(d_key, 4, 1)
        key_tiles += [d_key[:, :, :TILE], d_key[:, :, TILE:]]
    low = lax.broadcasted_iota(jnp.int32, (chips, 8, TILE), 1) < 4
    for c in range(2):
        a, b, e = key_tiles[3 * c : 3 * c + 3]
        mb[c, :, 144:160, :] = jnp.concatenate(
            [jnp.where(low, a, b), jnp.where(low, e, 0.0)], axis=1
        ).astype(jnp.bfloat16)

    swap_pair = remote(mb.at[other], pair, pair_sem.at[0], pair_sem.at[1], sibling)
    swap_pair.start()
    swap_pair.wait_recv()
    rs_sent = []
    for offset in range(1, chips):
        n, device = chip(offset)
        rs_out[offset - 1] = (
            mb[core, n].astype(jnp.float32) + pair[n].astype(jnp.float32)
        ).astype(jnp.bfloat16)
        copy = remote(
            rs_out.at[offset - 1], rs_in.at[offset - 1], rs_send.at[offset - 1],
            rs_recv.at[offset - 1], device,
        )
        copy.start()
        rs_sent.append(copy)

    for g in range(groups):
        cols = slice(g * 256, g * 256 + 256)
        gq_v[:, cols] = (dot(ds_s[g], kbd[g], TN) * scale).astype(jnp.bfloat16)
    stores = [pltpu.make_async_copy(gq_v, gq_hbm, out_sem.at[0])]
    stores[0].start()

    mine = mb[core, me].astype(jnp.float32) + pair[me].astype(jnp.float32)
    for offset in range(1, chips):
        rs_sent[offset - 1].wait_recv()
        mine = mine + rs_in[offset - 1].astype(jnp.float32)
    ag[core, me] = mine[:144].astype(jnp.bfloat16)
    dk[core] = mine[144:]
    ag_out = []
    for offset in range(1, chips):
        n, device = chip(offset)
        copy = remote(
            ag.at[core, me], ag.at[core, me], ag_send.at[offset - 1], ag_recv.at[offset - 1], device
        )
        copy.start()
        ag_out.append(copy)
    dk_copy = remote(dk.at[core], dk.at[core], dk_sem.at[0], dk_sem.at[1], sibling)
    dk_copy.start()
    fw_out = [remote(ag.at[core, me], ag.at[core, me], fw_send.at[0], fw_recv.at[0], sibling)]
    fw_out[0].start()
    for offset in range(1, chips):
        n, device = chip(chips - offset)
        remote(
            ag.at[core, n], ag.at[core, n], ag_send.at[offset - 1], ag_recv.at[offset - 1], device
        ).wait_recv()
        copy = remote(
            ag.at[core, n], ag.at[core, n], fw_send.at[offset], fw_recv.at[offset], sibling
        )
        copy.start()
        fw_out.append(copy)

    def arrived(offset):
        n, _ = chip(chips - offset)
        remote(
            ag.at[other, n], ag.at[other, n], fw_send.at[offset], fw_recv.at[offset], sibling
        ).wait_recv()

    remote(dk.at[other], dk.at[other], dk_sem.at[0], dk_sem.at[1], sibling).wait_recv()
    for c in range(2):
        for t in range(3):
            at = (c * 3 + t) * TILE
            gkv[0, :, at : at + TILE] = dk[c, t * 4 : t * 4 + 4, :]
    arrived(0)
    for g in range(groups):
        m_own = jnp.concatenate(
            [ag[c, me, t * 48 + g * 16 : t * 48 + g * 16 + 16, :] for c in range(2) for t in range(3)],
            axis=1,
        )
        r = jnp.where(diag[:16], dot(m_own, w[g * 256 : g * 256 + 256, :], NT), 0.0)
        r = r[:8] + r[8:]
        r = r + pltpu.roll(r, 4, 0)
        gkv[0, :, D + g * 256 : D + g * 256 + 256] = r[:4]

    for offset in range(1, chips):
        arrived(offset)
    for g in range(groups):
        m_g = jnp.concatenate(
            [
                ag[c, :, t * 48 + g * 16 : t * 48 + g * 16 + 16, :].reshape(krows, TILE)
                for c in range(2)
                for t in range(3)
            ],
            axis=1,
        )
        part = slice(g * 256, g * 256 + 256)
        gw_v[part, :] = dot(vbd[g], m_g, TN)
        store = pltpu.make_async_copy(gw_v.at[part], gw_hbm.at[part], out_sem.at[1 + g])
        store.start()
        stores.append(store)
    for copy in kv_out + [swap_pair] + rs_sent + ag_out + fw_out + [dk_copy]:
        copy.wait_send()
    for store in stores:
        store.wait()


def fused(xs, zs, query_heads, d_out, anchor_kv, point_counts, slot_car, out_weight):
    chips = xs * zs
    rows = query_heads.shape[0]
    bf, f32 = jnp.bfloat16, jnp.float32
    dma = lambda n: pltpu.SemaphoreType.DMA((n,))
    smem = pl.BlockSpec(memory_space=pltpu.SMEM)
    vmem = pl.BlockSpec(memory_space=pltpu.VMEM)
    anywhere = pl.BlockSpec(memory_space=pl.ANY)
    return pl.pallas_call(
        functools.partial(fused_kernel, xs, zs),
        out_shape=(
            jax.ShapeDtypeStruct((rows, D), bf),
            jax.ShapeDtypeStruct(anchor_kv.shape, f32),
            jax.ShapeDtypeStruct((D, D), f32),
        ),
        in_specs=[smem, smem, vmem, anywhere, anywhere, anywhere],
        out_specs=(anywhere, vmem, anywhere),
        scratch_shapes=[
            pltpu.VMEM((rows, D), bf),
            pltpu.VMEM((rows, D), bf),
            pltpu.VMEM((D, D), bf),
            pltpu.VMEM((48, TILE), f32),
            pltpu.VMEM((chips, 48, TILE), bf),
            pltpu.VMEM((rows, D), bf),
            pltpu.VMEM((3, chips * 16, 256), bf),
            pltpu.VMEM((3, chips * 16, 256), bf),
            pltpu.VMEM((chips * 16, rows), bf),
            pltpu.VMEM((3, chips * 16, rows), bf),
            pltpu.VMEM((rows, D), bf),
            pltpu.VMEM((D, D), f32),
            pltpu.VMEM((2, chips, 160, TILE), bf),
            pltpu.VMEM((chips, 160, TILE), bf),
            pltpu.VMEM((chips - 1, 160, TILE), bf),
            pltpu.VMEM((chips - 1, 160, TILE), bf),
            pltpu.VMEM((2, chips, 144, TILE), bf),
            pltpu.VMEM((2, 16, TILE), f32),
            dma(3),
            dma(4),
            dma(chips - 1),
            dma(chips - 1),
            dma(2),
            dma(chips - 1),
            dma(chips - 1),
            dma(chips - 1),
            dma(chips - 1),
            dma(chips),
            dma(chips),
            dma(2),
        ],
        compiler_params=pltpu.CompilerParams(
            collective_id=0, has_side_effects=True, vmem_limit_bytes=48 * 1024 * 1024
        ),
        cost_estimate=pl.CostEstimate(
            flops=2 * rows * D * D * 3, bytes_accessed=8 * 1024 * 1024, transcendentals=rows * 96
        ),
    )(point_counts, slot_car, anchor_kv, query_heads, d_out, out_weight)


def choose(mesh):
    xs, zs, cores = mesh.shape["query"], mesh.shape["car"], mesh.shape["replica"]

    def run(query_heads, d_out, anchor_kv, point_counts, slot_car, out_weight):
        args = (query_heads, d_out, anchor_kv, point_counts, slot_car, out_weight)
        few = xs * zs == 8 and cores == 2 and anchor_kv.shape[:2] == (1, 4)
        if few and query_heads.shape[0] % TILE == 0:
            return fused(xs, zs, *args)
        return body(*args)

    return run


def solution(mesh):
    in_specs = (
        P(("groups", "query", "car", "replica"), None),
        P(("groups", "query", "car", "replica"), None),
        P(("groups", "car"), "query", None),
        P(("groups", "query", "car", "replica"), None),
        P("groups"),
        P(),
    )
    out_specs = (
        P(("groups", "query", "car", "replica"), None),
        P(("groups", "car"), "query", None),
        P("groups", None),
    )
    return jax.shard_map(choose(mesh), mesh=mesh, in_specs=in_specs, out_specs=out_specs, check_vma=False)
```

```python
import functools
import math

import jax
import jax.numpy as jnp
from jax import lax
from jax.experimental import pallas as pl
from jax.experimental.pallas import tpu as pltpu
from jax.sharding import PartitionSpec as P

D = 768
HEADS = 12
HEAD_DIM = 64


def head_view(values):
    return values.reshape(values.shape[0], HEADS, HEAD_DIM)


def car_lookup(start, count, anchors_each, owners, slot_car):
    rows = start + jnp.arange(count, dtype=jnp.int32)
    slots = rows // anchors_each % owners
    table = slots[:, None] == jnp.arange(slot_car.shape[0], dtype=jnp.int32)[None, :]
    return jnp.sum(jnp.where(table, slot_car[None, :], 0), axis=1)


def body(query_heads, d_out, anchor_kv, point_counts, slot_car, out_weight):
    scale = HEAD_DIM ** (-0.5)
    owners = lax.axis_size("car")
    anchors_each = anchor_kv.shape[1]
    rows_here = query_heads.shape[0]
    ends = jnp.cumsum(point_counts[0])
    local = jnp.arange(rows_here, dtype=jnp.int32)
    point_car = jnp.sum((local[:, None] >= ends[None, :]).astype(jnp.int32), axis=1)
    panel = anchor_kv[0]
    queries = head_view(query_heads)

    def allowed_for(start, count):
        cars = car_lookup(start, count, anchors_each, owners, slot_car)
        return (point_car[:, None] == cars[None, :])[:, None, :]

    def forward_step(carry, piece, start):
        best, total, accum = carry
        count = piece.shape[0]
        keys = head_view(piece[:, :D])
        values = head_view(piece[:, D:])
        allowed = allowed_for(start, count)
        scores = (
            jnp.einsum("qhe,khe->qhk", queries, keys, preferred_element_type=jnp.float32) * scale
        )
        peak = jnp.max(jnp.where(allowed, scores, -1e30), axis=2)
        new_best = jnp.maximum(best, peak)
        weights = jnp.where(allowed, jnp.exp(scores - new_best[:, :, None]), 0.0)
        fade = jnp.exp(best - new_best)
        total = total * fade + jnp.sum(weights, axis=2)
        accum = accum * fade[:, :, None] + jnp.einsum(
            "qhk,khe->qhe", weights.astype(jnp.bfloat16), values, preferred_element_type=jnp.float32
        )
        return (new_best, total, accum)

    init = (
        jnp.full((rows_here, HEADS), -1e30, jnp.float32),
        jnp.zeros((rows_here, HEADS), jnp.float32),
        jnp.zeros((rows_here, HEADS, HEAD_DIM), jnp.float32),
    )
    kv_all = lax.all_gather(panel, ("query", "car"), axis=0, tiled=True)
    key_rows = kv_all.shape[0]
    block = math.gcd(key_rows, 128)
    blocks = kv_all.reshape(key_rows // block, block, 2 * D)

    def scan_forward(carry, inputs):
        piece, number = inputs
        return (forward_step(carry, piece, number * block), None)

    (best, total, accum), _ = lax.scan(
        scan_forward, init, (blocks, jnp.arange(key_rows // block, dtype=jnp.int32))
    )
    numbers = jnp.arange(key_rows // block, dtype=jnp.int32)
    attended = (accum / total[:, :, None]).reshape(rows_here, D).astype(jnp.bfloat16)
    d_att = lax.dot_general(
        d_out, out_weight, (((1,), (1,)), ((), ())), preferred_element_type=jnp.float32
    ).astype(jnp.bfloat16)
    weight_term = lax.dot_general(
        attended, d_out, (((0,), (0,)), ((), ())), preferred_element_type=jnp.float32
    )
    weight_grad = lax.psum(weight_term, ("query", "car", "replica"))
    d_heads = head_view(d_att)
    delta = jnp.sum(d_heads.astype(jnp.float32) * head_view(attended).astype(jnp.float32), axis=2)

    def backward_step(d_query, inputs):
        piece, number = inputs
        keys = head_view(piece[:, :D])
        values = head_view(piece[:, D:])
        allowed = allowed_for(number * block, block)
        scores = (
            jnp.einsum("qhe,khe->qhk", queries, keys, preferred_element_type=jnp.float32) * scale
        )
        prob = jnp.where(allowed, jnp.exp(scores - best[:, :, None]), 0.0) / total[:, :, None]
        d_prob = jnp.einsum("qhe,khe->qhk", d_heads, values, preferred_element_type=jnp.float32)
        d_score = (prob * (d_prob - delta[:, :, None])).astype(jnp.bfloat16)
        d_query = d_query + jnp.einsum(
            "qhk,khe->qhe", d_score, keys, preferred_element_type=jnp.float32
        )
        d_key = (
            jnp.einsum("qhk,qhe->khe", d_score, queries, preferred_element_type=jnp.float32) * scale
        )
        d_value = jnp.einsum(
            "qhk,qhe->khe", prob.astype(jnp.bfloat16), d_heads, preferred_element_type=jnp.float32
        )
        return (
            d_query,
            jnp.concatenate([d_key.reshape(block, D), d_value.reshape(block, D)], axis=1),
        )

    d_query, stacked = lax.scan(
        backward_step, jnp.zeros((rows_here, HEADS, HEAD_DIM), jnp.float32), (blocks, numbers)
    )
    kv_term = stacked.reshape(key_rows, 2 * D)
    kv_part = lax.psum_scatter(kv_term, ("query", "car"), scatter_dimension=0, tiled=True)
    kv_mine = lax.psum(kv_part, "replica")
    grad_queries = (d_query * scale).reshape(rows_here, D).astype(jnp.bfloat16)
    return (grad_queries, kv_mine.reshape(1, anchors_each, 2 * D), weight_grad)


TILE = 128
GROUP = 4
NT = (((1,), (1,)), ((), ()))
TN = (((0,), (0,)), ((), ()))


def dot(a, b, dims=(((1,), (0,)), ((), ()))):
    return lax.dot_general(a, b, dims, preferred_element_type=jnp.float32)


def fused_kernel(
    xs, zs, counts_hbm, slots_hbm, kv, q_hbm, do_hbm, w_hbm, ag_hbm, gkv_hbm, kbd_hbm, vbd_hbm, ds_hbm,
    counts, slots, q, do, w, pack, kvall, da, kbd, vbd, prob_s, ds_s, mb, pair, x_out, x_in, z_out,
    z_in, ag, dk, gkv, in_sem, kv_send, kv_recv, pair_sem, x_send, x_recv, z_send, z_recv, agz_send,
    agz_recv, agx_send, agx_recv, fw_send, fw_recv, dk_sem, out_sem, piece_sem,
):
    scale = HEAD_DIM ** (-0.5)
    chips = xs * zs
    groups = HEADS // GROUP
    rows = q.shape[0]
    grp, x, z, core = (lax.axis_index(a) for a in ("groups", "query", "car", "replica"))
    me = x * zs + z
    other = 1 - core
    sibling = (grp, x, z, other)
    across = (grp, 1 - x, z, core)
    stores = []

    def store(src, dst, sem):
        copy = pltpu.make_async_copy(src, dst, sem)
        copy.start()
        stores.append(copy)

    def along(offset):
        to = lax.rem(z + offset, zs)
        return to, (grp, x, to, core)

    def chip(offset):
        n = lax.rem(me + offset, chips)
        return n, (grp, n // zs, lax.rem(n, zs), core)

    def remote(src, dst, send, recv, device):
        return pltpu.make_async_remote_copy(
            src_ref=src, dst_ref=dst, send_sem=send, recv_sem=recv, device_id=device,
            device_id_type=pl.DeviceIdType.MESH,
        )

    loads = [
        pltpu.make_async_copy(a, b, in_sem.at[i])
        for i, (a, b) in enumerate(((do_hbm, do), (w_hbm, w), (q_hbm, q), (counts_hbm, counts), (slots_hbm, slots)))
    ]
    for load in loads:
        load.start()

    barrier = pltpu.get_barrier_semaphore()
    for offset in range(1, chips):
        pl.semaphore_signal(
            barrier, inc=1, device_id=chip(offset)[1], device_id_type=pl.DeviceIdType.MESH
        )
    pl.semaphore_signal(barrier, inc=1, device_id=sibling, device_id_type=pl.DeviceIdType.MESH)

    own_kv = kv[0].astype(jnp.float32)
    for h in range(HEADS):
        pack[h * 4 : h * 4 + 4, :HEAD_DIM] = own_kv[:, h * HEAD_DIM : (h + 1) * HEAD_DIM]
        pack[h * 4 : h * 4 + 4, HEAD_DIM:] = own_kv[:, D + h * HEAD_DIM : D + (h + 1) * HEAD_DIM]
    kvall[me] = pack[...].astype(jnp.bfloat16)

    pl.semaphore_wait(barrier, chips)
    kv_out = []
    for offset in range(1, chips):
        n, device = chip(offset)
        copy = remote(
            kvall.at[me], kvall.at[me], kv_send.at[offset - 1], kv_recv.at[offset - 1], device
        )
        copy.start()
        kv_out.append(copy)

    loads[0].wait()
    loads[1].wait()
    for g in range(groups):
        cols = slice(g * 256, g * 256 + 256)
        da[:, cols] = dot(do[...], w[cols, :], NT).astype(jnp.bfloat16)
    for load in loads[2:]:
        load.wait()

    lane = lax.broadcasted_iota(jnp.int32, (8, rows), 1)
    sub = lax.broadcasted_iota(jnp.int32, (8, rows), 0)
    masks = []
    for s in range(zs):
        car = slots[s]
        first = jnp.int32(0)
        size = jnp.int32(0)
        for c in range(counts.shape[1]):
            first = first + jnp.where(c < car, counts[0, c], 0)
            size = size + jnp.where(c == car, counts[0, c], 0)
        masks.append((lane >= first) & (lane < first + size))

    def swap(v, s):
        return jnp.where((sub & s) == 0, pltpu.roll(v, 8 - s, 0), pltpu.roll(v, s, 0))

    def over_four(v, op):
        v = op(v, swap(v, 1))
        return op(v, swap(v, 2))

    def pick(full, xi, hp):
        part = [full[(xi * zs + s) * 16 + hp * 8 : (xi * zs + s) * 16 + hp * 8 + 8, :] for s in range(zs)]
        out = part[0]
        for s in range(1, zs):
            out = jnp.where(masks[s], part[s], out)
        return out

    for offset in range(1, chips):
        n, device = chip(chips - offset)
        remote(
            kvall.at[n], kvall.at[n], kv_send.at[offset - 1], kv_recv.at[offset - 1], device
        ).wait_recv()

    krows = chips * 16
    diag_row = lax.broadcasted_iota(jnp.int32, (krows, 256), 0) // 4 % GROUP
    diag = diag_row == lax.broadcasted_iota(jnp.int32, (krows, 256), 1) // HEAD_DIM
    half = lax.broadcasted_iota(jnp.int32, (krows, TILE), 1) < HEAD_DIM
    key_tiles = []
    for g in range(groups):
        cols = slice(g * 256, g * 256 + 256)
        both = kvall[:, g * 16 : g * 16 + 16, :].reshape(krows, TILE).astype(jnp.float32)
        turned = pltpu.roll(both, HEAD_DIM, 1)
        keys2 = jnp.where(half, both, turned)
        vals2 = jnp.where(half, turned, both)
        kd = jnp.where(diag, jnp.concatenate([keys2, keys2], axis=1), 0.0).astype(jnp.bfloat16)
        vd = jnp.where(diag, jnp.concatenate([vals2, vals2], axis=1), 0.0).astype(jnp.bfloat16)
        kbd[g] = kd
        vbd[g] = vd
        scores = dot(kd, q[:, cols], NT)
        d_prob = dot(vd, da[:, cols], NT)
        probs = [[None, None] for _ in range(xs)]
        dss = [[None, None] for _ in range(xs)]
        for hp in range(2):
            sc = [pick(scores, xi, hp) * scale for xi in range(xs)]
            dp = [pick(d_prob, xi, hp) for xi in range(xs)]
            best = over_four(functools.reduce(jnp.maximum, sc), jnp.maximum)
            wt = [jnp.exp(v - best) for v in sc]
            total = over_four(functools.reduce(jnp.add, wt), jnp.add)
            inv = 1.0 / total
            pr = [v * inv for v in wt]
            delta = over_four(functools.reduce(jnp.add, [a * b for a, b in zip(pr, dp)]), jnp.add)
            for xi in range(xs):
                probs[xi][hp] = pr[xi]
                dss[xi][hp] = pr[xi] * (dp[xi] - delta)
        for xi in range(xs):
            for s in range(zs):
                at = slice((xi * zs + s) * 16, (xi * zs + s) * 16 + 16)
                mask = jnp.concatenate([masks[s], masks[s]], axis=0)
                prob_s[at, :] = jnp.where(mask, jnp.concatenate(probs[xi], axis=0), 0.0).astype(
                    jnp.bfloat16
                )
                ds_s[g, at, :] = jnp.where(mask, jnp.concatenate(dss[xi], axis=0), 0.0).astype(
                    jnp.bfloat16
                )
        term = dot(prob_s[...], do[...]).astype(jnp.bfloat16)
        for c in range(2):
            for t in range(3):
                at = (c * 3 + t) * TILE
                mb[c, :, t * 48 + g * 16 : t * 48 + g * 16 + 16, :] = term[
                    :, at : at + TILE
                ].reshape(chips, 16, TILE)
        d_key = jnp.where(diag, dot(ds_s[g], q[:, cols]), 0.0) * scale
        d_key = d_key.reshape(chips, 2, 8, 256)
        d_key = d_key[:, 0] + d_key[:, 1]
        d_key = d_key + pltpu.roll(d_key, 4, 1)
        key_tiles += [d_key[:, :, :TILE], d_key[:, :, TILE:]]
    low = lax.broadcasted_iota(jnp.int32, (chips, 8, TILE), 1) < 4
    for c in range(2):
        a, b, e = key_tiles[3 * c : 3 * c + 3]
        mb[c, :, 144:160, :] = jnp.concatenate(
            [jnp.where(low, a, b), jnp.where(low, e, 0.0)], axis=1
        ).astype(jnp.bfloat16)

    swap_pair = remote(mb.at[other], pair, pair_sem.at[0], pair_sem.at[1], sibling)
    swap_pair.start()
    store(kbd, kbd_hbm, out_sem.at[0])
    store(vbd, vbd_hbm, out_sem.at[1])
    store(ds_s, ds_hbm, out_sem.at[2])
    swap_pair.wait_recv()
    x_sent, z_sent = [], []
    order = list(range(1, zs)) + [0]

    def summed(n):
        return mb[core, n].astype(jnp.float32) + pair[n].astype(jnp.float32)

    for o in order:
        x_out[o] = summed((1 - x) * zs + along(o)[0]).astype(jnp.bfloat16)
        copy = remote(x_out.at[o], x_in.at[o], x_send.at[o], x_recv.at[o], across)
        copy.start()
        x_sent.append(copy)
    for i, o in enumerate(order[:-1]):
        to, device = along(o)
        x_sent[i].wait_recv()
        z_out[o - 1] = (
            summed(x * zs + to) + x_in[o].astype(jnp.float32)
        ).astype(jnp.bfloat16)
        copy = remote(
            z_out.at[o - 1], z_in.at[o - 1], z_send.at[o - 1], z_recv.at[o - 1], device
        )
        copy.start()
        z_sent.append(copy)
    x_sent[-1].wait_recv()
    mine = summed(me) + x_in[0].astype(jnp.float32)
    for copy in z_sent:
        copy.wait_recv()
    for o in range(1, zs):
        mine = mine + z_in[o - 1].astype(jnp.float32)
    ag[core, me] = mine[:144].astype(jnp.bfloat16)
    dk[core] = mine[144:]
    agz_out, agx_out, fw_out = [], [], []
    for o in range(1, zs):
        copy = remote(
            ag.at[core, me], ag.at[core, me], agz_send.at[o - 1], agz_recv.at[o - 1], along(o)[1]
        )
        copy.start()
        agz_out.append(copy)

    def to_across(o):
        n = x * zs + along(zs - o)[0]
        copy = remote(ag.at[core, n], ag.at[core, n], agx_send.at[o], agx_recv.at[o], across)
        copy.start()
        agx_out.append(copy)

    def piece(i):
        return (x if i < zs else 1 - x) * zs + along(zs - i % zs)[0]

    def to_sibling(i):
        n = piece(i)
        copy = remote(ag.at[core, n], ag.at[core, n], fw_send.at[i], fw_recv.at[i], sibling)
        copy.start()
        fw_out.append(copy)
        store(ag.at[core, n], ag_hbm.at[core, n], piece_sem.at[0, i])

    def arrived(i):
        n = piece(i)
        remote(
            ag.at[other, n], ag.at[other, n], fw_send.at[i], fw_recv.at[i], sibling
        ).wait_recv()
        store(ag.at[other, n], ag_hbm.at[other, n], piece_sem.at[1, i])

    to_across(0)
    dk_copy = remote(dk.at[core], dk.at[core], dk_sem.at[0], dk_sem.at[1], sibling)
    dk_copy.start()
    to_sibling(0)
    for o in range(1, zs):
        n = piece(o)
        remote(
            ag.at[core, n], ag.at[core, n], agz_send.at[o - 1], agz_recv.at[o - 1], along(o)[1]
        ).wait_recv()
        to_across(o)
        to_sibling(o)

    def from_across(o):
        n = piece(zs + o)
        remote(
            ag.at[core, n], ag.at[core, n], agx_send.at[o], agx_recv.at[o], across
        ).wait_recv()
        to_sibling(zs + o)

    remote(dk.at[other], dk.at[other], dk_sem.at[0], dk_sem.at[1], sibling).wait_recv()
    for c in range(2):
        for t in range(3):
            at = (c * 3 + t) * TILE
            gkv[:, at : at + TILE] = dk[c, t * 4 : t * 4 + 4, :]
    arrived(0)
    for g in range(groups):
        m_own = jnp.concatenate(
            [ag[c, me, t * 48 + g * 16 : t * 48 + g * 16 + 16, :] for c in range(2) for t in range(3)],
            axis=1,
        )
        r = jnp.where(diag[:16], dot(m_own, w[g * 256 : g * 256 + 256, :], NT), 0.0)
        r = r[:8] + r[8:]
        r = r + pltpu.roll(r, 4, 0)
        gkv[:, D + g * 256 : D + g * 256 + 256] = r[:4]
    store(gkv, gkv_hbm.at[0], out_sem.at[3])

    for o in range(zs):
        from_across(o)
    for i in range(1, 2 * zs):
        arrived(i)
    for copy in kv_out + [swap_pair] + x_sent + z_sent + agz_out + agx_out + fw_out + [dk_copy]:
        copy.wait_send()
    for copy in stores:
        copy.wait()


def last_kernel(
    ag_hbm, gkv_hbm, kbd_hbm, vbd_hbm, ds_hbm, gq_out, gkv_out, gw_out,
    ag, kbd, vbd, ds_s, gq, gw, in_sem, out_sem,
):
    scale = HEAD_DIM ** (-0.5)
    krows = kbd.shape[1]
    groups = HEADS // GROUP
    loads = [
        pltpu.make_async_copy(a, b, in_sem.at[i])
        for i, (a, b) in enumerate(((ds_hbm, ds_s), (kbd_hbm, kbd), (vbd_hbm, vbd), (ag_hbm, ag)))
    ]
    for load in loads:
        load.start()
    stores = [pltpu.make_async_copy(gkv_hbm, gkv_out, out_sem.at[0])]
    stores[0].start()
    loads[0].wait()
    loads[1].wait()
    for g in range(groups):
        cols = slice(g * 256, g * 256 + 256)
        gq[:, cols] = (dot(ds_s[g], kbd[g], TN) * scale).astype(jnp.bfloat16)
    stores.append(pltpu.make_async_copy(gq, gq_out, out_sem.at[1]))
    stores[1].start()
    loads[2].wait()
    loads[3].wait()
    for g in range(groups):
        m_g = jnp.concatenate(
            [
                ag[c, :, t * 48 + g * 16 : t * 48 + g * 16 + 16, :].reshape(krows, TILE)
                for c in range(2)
                for t in range(3)
            ],
            axis=1,
        )
        part = slice(g * 256, g * 256 + 256)
        gw[part, :] = dot(vbd[g], m_g, TN)
        stores.append(pltpu.make_async_copy(gw.at[part], gw_out.at[part], out_sem.at[2 + g]))
        stores[-1].start()
    for copy in stores:
        copy.wait()


def fused(xs, zs, query_heads, d_out, anchor_kv, point_counts, slot_car, out_weight):
    chips = xs * zs
    rows = query_heads.shape[0]
    bf, f32 = jnp.bfloat16, jnp.float32
    dma = lambda n: pltpu.SemaphoreType.DMA((n,))
    hbm = pl.BlockSpec(memory_space=pltpu.HBM)
    vmem = pl.BlockSpec(memory_space=pltpu.VMEM)
    limit = 60 * 1024 * 1024
    half_shape = (chips, 160, TILE)
    kd_shape = (3, chips * 16, 256)
    ds_shape = (3, chips * 16, rows)
    ag_shape = (2, chips, 144, TILE)
    mids = pl.pallas_call(
        functools.partial(fused_kernel, xs, zs),
        out_shape=(
            jax.ShapeDtypeStruct(ag_shape, bf),
            jax.ShapeDtypeStruct(anchor_kv.shape, f32),
            jax.ShapeDtypeStruct(kd_shape, bf),
            jax.ShapeDtypeStruct(kd_shape, bf),
            jax.ShapeDtypeStruct(ds_shape, bf),
        ),
        in_specs=[hbm, hbm, vmem, hbm, hbm, hbm],
        out_specs=(hbm,) * 5,
        scratch_shapes=[
            pltpu.SMEM(point_counts.shape, jnp.int32),
            pltpu.SMEM(slot_car.shape, jnp.int32),
            pltpu.VMEM((rows, D), bf),
            pltpu.VMEM((rows, D), bf),
            pltpu.VMEM((D, D), bf),
            pltpu.VMEM((48, TILE), f32),
            pltpu.VMEM((chips, 48, TILE), bf),
            pltpu.VMEM((rows, D), bf),
            pltpu.VMEM(kd_shape, bf),
            pltpu.VMEM(kd_shape, bf),
            pltpu.VMEM((chips * 16, rows), bf),
            pltpu.VMEM(ds_shape, bf),
            pltpu.VMEM((2,) + half_shape, bf),
            pltpu.VMEM(half_shape, bf),
            pltpu.VMEM((zs, 160, TILE), bf),
            pltpu.VMEM((zs, 160, TILE), bf),
            pltpu.VMEM((zs - 1, 160, TILE), bf),
            pltpu.VMEM((zs - 1, 160, TILE), bf),
            pltpu.VMEM(ag_shape, bf),
            pltpu.VMEM((2, 16, TILE), f32),
            pltpu.VMEM(anchor_kv.shape[1:], f32),
            dma(5),
            dma(chips - 1),
            dma(chips - 1),
            dma(2),
            dma(zs),
            dma(zs),
            dma(zs - 1),
            dma(zs - 1),
            dma(zs - 1),
            dma(zs - 1),
            dma(zs),
            dma(zs),
            dma(chips),
            dma(chips),
            dma(2),
            dma(4),
            pltpu.SemaphoreType.DMA((2, chips)),
        ],
        compiler_params=pltpu.CompilerParams(
            collective_id=0, has_side_effects=True, vmem_limit_bytes=limit
        ),
        cost_estimate=pl.CostEstimate(
            flops=2 * rows * D * D * 2, bytes_accessed=5 * 1024 * 1024, transcendentals=rows * 96
        ),
    )(point_counts, slot_car, anchor_kv, query_heads, d_out, out_weight)
    return pl.pallas_call(
        last_kernel,
        out_shape=(
            jax.ShapeDtypeStruct((rows, D), bf),
            jax.ShapeDtypeStruct(anchor_kv.shape, f32),
            jax.ShapeDtypeStruct((D, D), f32),
        ),
        in_specs=[hbm] * 5,
        out_specs=(hbm,) * 3,
        scratch_shapes=[
            pltpu.VMEM(ag_shape, bf),
            pltpu.VMEM(kd_shape, bf),
            pltpu.VMEM(kd_shape, bf),
            pltpu.VMEM(ds_shape, bf),
            pltpu.VMEM((rows, D), bf),
            pltpu.VMEM((D, D), f32),
            dma(4),
            dma(5),
        ],
        compiler_params=pltpu.CompilerParams(vmem_limit_bytes=limit),
        cost_estimate=pl.CostEstimate(
            flops=2 * rows * D * D, bytes_accessed=5 * 1024 * 1024, transcendentals=0
        ),
    )(*mids)


def choose(mesh):
    xs, zs, cores = mesh.shape["query"], mesh.shape["car"], mesh.shape["replica"]

    def run(query_heads, d_out, anchor_kv, point_counts, slot_car, out_weight):
        args = (query_heads, d_out, anchor_kv, point_counts, slot_car, out_weight)
        few = xs * zs == 8 and cores == 2 and anchor_kv.shape[:2] == (1, 4)
        if few and query_heads.shape[0] % TILE == 0:
            return fused(xs, zs, *args)
        return body(*args)

    return run


def solution(mesh):
    in_specs = (
        P(("groups", "query", "car", "replica"), None),
        P(("groups", "query", "car", "replica"), None),
        P(("groups", "car"), "query", None),
        P(("groups", "query", "car", "replica"), None),
        P("groups"),
        P(),
    )
    out_specs = (
        P(("groups", "query", "car", "replica"), None),
        P(("groups", "car"), "query", None),
        P("groups", None),
    )
    return jax.shard_map(choose(mesh), mesh=mesh, in_specs=in_specs, out_specs=out_specs, check_vma=False)
```

```python
import functools
import math

import jax
import jax.numpy as jnp
from jax import lax
from jax.experimental import pallas as pl
from jax.experimental.pallas import tpu as pltpu
from jax.sharding import PartitionSpec as P

D = 768
HEADS = 12
HEAD_DIM = 64


def head_view(values):
    return values.reshape(values.shape[0], HEADS, HEAD_DIM)


def car_lookup(start, count, anchors_each, owners, slot_car):
    rows = start + jnp.arange(count, dtype=jnp.int32)
    slots = rows // anchors_each % owners
    table = slots[:, None] == jnp.arange(slot_car.shape[0], dtype=jnp.int32)[None, :]
    return jnp.sum(jnp.where(table, slot_car[None, :], 0), axis=1)


def body(query_heads, d_out, anchor_kv, point_counts, slot_car, out_weight):
    scale = HEAD_DIM ** (-0.5)
    owners = lax.axis_size("car")
    anchors_each = anchor_kv.shape[1]
    rows_here = query_heads.shape[0]
    ends = jnp.cumsum(point_counts[0])
    local = jnp.arange(rows_here, dtype=jnp.int32)
    point_car = jnp.sum((local[:, None] >= ends[None, :]).astype(jnp.int32), axis=1)
    panel = anchor_kv[0]
    queries = head_view(query_heads)

    def allowed_for(start, count):
        cars = car_lookup(start, count, anchors_each, owners, slot_car)
        return (point_car[:, None] == cars[None, :])[:, None, :]

    def forward_step(carry, piece, start):
        best, total, accum = carry
        count = piece.shape[0]
        keys = head_view(piece[:, :D])
        values = head_view(piece[:, D:])
        allowed = allowed_for(start, count)
        scores = (
            jnp.einsum("qhe,khe->qhk", queries, keys, preferred_element_type=jnp.float32) * scale
        )
        peak = jnp.max(jnp.where(allowed, scores, -1e30), axis=2)
        new_best = jnp.maximum(best, peak)
        weights = jnp.where(allowed, jnp.exp(scores - new_best[:, :, None]), 0.0)
        fade = jnp.exp(best - new_best)
        total = total * fade + jnp.sum(weights, axis=2)
        accum = accum * fade[:, :, None] + jnp.einsum(
            "qhk,khe->qhe", weights.astype(jnp.bfloat16), values, preferred_element_type=jnp.float32
        )
        return (new_best, total, accum)

    init = (
        jnp.full((rows_here, HEADS), -1e30, jnp.float32),
        jnp.zeros((rows_here, HEADS), jnp.float32),
        jnp.zeros((rows_here, HEADS, HEAD_DIM), jnp.float32),
    )
    kv_all = lax.all_gather(panel, ("query", "car"), axis=0, tiled=True)
    key_rows = kv_all.shape[0]
    block = math.gcd(key_rows, 128)
    blocks = kv_all.reshape(key_rows // block, block, 2 * D)

    def scan_forward(carry, inputs):
        piece, number = inputs
        return (forward_step(carry, piece, number * block), None)

    (best, total, accum), _ = lax.scan(
        scan_forward, init, (blocks, jnp.arange(key_rows // block, dtype=jnp.int32))
    )
    numbers = jnp.arange(key_rows // block, dtype=jnp.int32)
    attended = (accum / total[:, :, None]).reshape(rows_here, D).astype(jnp.bfloat16)
    d_att = lax.dot_general(
        d_out, out_weight, (((1,), (1,)), ((), ())), preferred_element_type=jnp.float32
    ).astype(jnp.bfloat16)
    weight_term = lax.dot_general(
        attended, d_out, (((0,), (0,)), ((), ())), preferred_element_type=jnp.float32
    )
    weight_grad = lax.psum(weight_term, ("query", "car", "replica"))
    d_heads = head_view(d_att)
    delta = jnp.sum(d_heads.astype(jnp.float32) * head_view(attended).astype(jnp.float32), axis=2)

    def backward_step(d_query, inputs):
        piece, number = inputs
        keys = head_view(piece[:, :D])
        values = head_view(piece[:, D:])
        allowed = allowed_for(number * block, block)
        scores = (
            jnp.einsum("qhe,khe->qhk", queries, keys, preferred_element_type=jnp.float32) * scale
        )
        prob = jnp.where(allowed, jnp.exp(scores - best[:, :, None]), 0.0) / total[:, :, None]
        d_prob = jnp.einsum("qhe,khe->qhk", d_heads, values, preferred_element_type=jnp.float32)
        d_score = (prob * (d_prob - delta[:, :, None])).astype(jnp.bfloat16)
        d_query = d_query + jnp.einsum(
            "qhk,khe->qhe", d_score, keys, preferred_element_type=jnp.float32
        )
        d_key = (
            jnp.einsum("qhk,qhe->khe", d_score, queries, preferred_element_type=jnp.float32) * scale
        )
        d_value = jnp.einsum(
            "qhk,qhe->khe", prob.astype(jnp.bfloat16), d_heads, preferred_element_type=jnp.float32
        )
        return (
            d_query,
            jnp.concatenate([d_key.reshape(block, D), d_value.reshape(block, D)], axis=1),
        )

    d_query, stacked = lax.scan(
        backward_step, jnp.zeros((rows_here, HEADS, HEAD_DIM), jnp.float32), (blocks, numbers)
    )
    kv_term = stacked.reshape(key_rows, 2 * D)
    kv_part = lax.psum_scatter(kv_term, ("query", "car"), scatter_dimension=0, tiled=True)
    kv_mine = lax.psum(kv_part, "replica")
    grad_queries = (d_query * scale).reshape(rows_here, D).astype(jnp.bfloat16)
    return (grad_queries, kv_mine.reshape(1, anchors_each, 2 * D), weight_grad)


TILE = 128
GROUP = 4
NT = (((1,), (1,)), ((), ()))
TN = (((0,), (0,)), ((), ()))


def dot(a, b, dims=(((1,), (0,)), ((), ()))):
    return lax.dot_general(a, b, dims, preferred_element_type=jnp.float32)


def fused_kernel(
    xs, zs, counts_hbm, slots_hbm, kv, q_hbm, do_hbm, w_hbm, ag_hbm, gkv_hbm, kbd_hbm, vbd_hbm, ds_hbm,
    counts, slots, q, do, w, pack, kvall, da, kbd, vbd, prob_s, ds_s, mb, pair, x_out, x_in, z_out,
    z_in, ag, dk, gkv, in_sem, kv_send, kv_recv, pair_sem, x_send, x_recv, z_send, z_recv, agz_send,
    agz_recv, agx_send, agx_recv, fw_send, fw_recv, dk_sem, out_sem,
):
    scale = HEAD_DIM ** (-0.5)
    chips = xs * zs
    groups = HEADS // GROUP
    rows = q.shape[0]
    grp, x, z, core = (lax.axis_index(a) for a in ("groups", "query", "car", "replica"))
    me = x * zs + z
    other = 1 - core
    sibling = (grp, x, z, other)
    across = (grp, 1 - x, z, core)
    stores = []

    def store(src, dst, sem):
        copy = pltpu.make_async_copy(src, dst, sem)
        copy.start()
        stores.append(copy)

    def along(offset):
        to = line[offset % zs]
        return to, (grp, x, to, core)

    line = [z] + [lax.rem(z + offset, zs) for offset in range(1, zs)]

    def chip(offset):
        to_x = x if offset % chips < zs else 1 - x
        to_z = line[offset % zs]
        return to_x * zs + to_z, (grp, to_x, to_z, core)

    def source(offset):
        to_x = x if offset < zs else 1 - x
        return to_x * zs + line[(zs - offset % zs) % zs]

    def remote(src, dst, send, recv, device):
        return pltpu.make_async_remote_copy(
            src_ref=src, dst_ref=dst, send_sem=send, recv_sem=recv, device_id=device,
            device_id_type=pl.DeviceIdType.MESH,
        )

    loads = [
        pltpu.make_async_copy(a, b, in_sem.at[i])
        for i, (a, b) in enumerate(((do_hbm, do), (w_hbm, w), (q_hbm, q), (counts_hbm, counts), (slots_hbm, slots)))
    ]
    for load in loads:
        load.start()

    barrier = pltpu.get_barrier_semaphore()
    for offset in range(1, chips):
        pl.semaphore_signal(
            barrier, inc=1, device_id=chip(offset)[1], device_id_type=pl.DeviceIdType.MESH
        )
    pl.semaphore_signal(barrier, inc=1, device_id=sibling, device_id_type=pl.DeviceIdType.MESH)

    own_kv = kv[0].astype(jnp.float32)
    for h in range(HEADS):
        pack[h * 4 : h * 4 + 4, :HEAD_DIM] = own_kv[:, h * HEAD_DIM : (h + 1) * HEAD_DIM]
        pack[h * 4 : h * 4 + 4, HEAD_DIM:] = own_kv[:, D + h * HEAD_DIM : D + (h + 1) * HEAD_DIM]
    kvall[me] = pack[...].astype(jnp.bfloat16)

    pl.semaphore_wait(barrier, chips)
    kv_out = []
    for offset in range(1, chips):
        n, device = chip(offset)
        copy = remote(
            kvall.at[me], kvall.at[me], kv_send.at[offset - 1], kv_recv.at[offset - 1], device
        )
        copy.start()
        kv_out.append(copy)

    loads[0].wait()
    loads[1].wait()
    for g in range(groups):
        cols = slice(g * 256, g * 256 + 256)
        da[:, cols] = dot(do[...], w[cols, :], NT).astype(jnp.bfloat16)
    for load in loads[2:]:
        load.wait()

    lane = lax.broadcasted_iota(jnp.int32, (8, rows), 1)
    sub = lax.broadcasted_iota(jnp.int32, (8, rows), 0)
    masks = []
    for s in range(zs):
        car = slots[s]
        first = jnp.int32(0)
        size = jnp.int32(0)
        for c in range(counts.shape[1]):
            first = first + jnp.where(c < car, counts[0, c], 0)
            size = size + jnp.where(c == car, counts[0, c], 0)
        masks.append((lane >= first) & (lane < first + size))

    def swap(v, s):
        return jnp.where((sub & s) == 0, pltpu.roll(v, 8 - s, 0), pltpu.roll(v, s, 0))

    def over_four(v, op):
        v = op(v, swap(v, 1))
        return op(v, swap(v, 2))

    def pick(full, xi, hp):
        part = [full[(xi * zs + s) * 16 + hp * 8 : (xi * zs + s) * 16 + hp * 8 + 8, :] for s in range(zs)]
        out = part[0]
        for s in range(1, zs):
            out = jnp.where(masks[s], part[s], out)
        return out

    for offset in range(1, chips):
        n, device = source(offset), across
        remote(
            kvall.at[n], kvall.at[n], kv_send.at[offset - 1], kv_recv.at[offset - 1], device
        ).wait_recv()

    krows = chips * 16
    diag_row = lax.broadcasted_iota(jnp.int32, (krows, 256), 0) // 4 % GROUP
    diag = diag_row == lax.broadcasted_iota(jnp.int32, (krows, 256), 1) // HEAD_DIM
    half = lax.broadcasted_iota(jnp.int32, (krows, TILE), 1) < HEAD_DIM
    key_tiles = []
    for g in range(groups):
        cols = slice(g * 256, g * 256 + 256)
        both = kvall[:, g * 16 : g * 16 + 16, :].reshape(krows, TILE).astype(jnp.float32)
        turned = pltpu.roll(both, HEAD_DIM, 1)
        keys2 = jnp.where(half, both, turned)
        vals2 = jnp.where(half, turned, both)
        kd = jnp.where(diag, jnp.concatenate([keys2, keys2], axis=1), 0.0).astype(jnp.bfloat16)
        vd = jnp.where(diag, jnp.concatenate([vals2, vals2], axis=1), 0.0).astype(jnp.bfloat16)
        kbd[g] = kd
        vbd[g] = vd
        scores = dot(kd, q[:, cols], NT)
        d_prob = dot(vd, da[:, cols], NT)
        probs = [[None, None] for _ in range(xs)]
        dss = [[None, None] for _ in range(xs)]
        for hp in range(2):
            sc = [pick(scores, xi, hp) * scale for xi in range(xs)]
            dp = [pick(d_prob, xi, hp) for xi in range(xs)]
            best = over_four(functools.reduce(jnp.maximum, sc), jnp.maximum)
            wt = [jnp.exp(v - best) for v in sc]
            total = over_four(functools.reduce(jnp.add, wt), jnp.add)
            inv = 1.0 / total
            pr = [v * inv for v in wt]
            delta = over_four(functools.reduce(jnp.add, [a * b for a, b in zip(pr, dp)]), jnp.add)
            for xi in range(xs):
                probs[xi][hp] = pr[xi]
                dss[xi][hp] = pr[xi] * (dp[xi] - delta)
        for xi in range(xs):
            for s in range(zs):
                at = slice((xi * zs + s) * 16, (xi * zs + s) * 16 + 16)
                mask = jnp.concatenate([masks[s], masks[s]], axis=0)
                prob_s[at, :] = jnp.where(mask, jnp.concatenate(probs[xi], axis=0), 0.0).astype(
                    jnp.bfloat16
                )
                ds_s[g, at, :] = jnp.where(mask, jnp.concatenate(dss[xi], axis=0), 0.0).astype(
                    jnp.bfloat16
                )
        term = dot(prob_s[...], do[...]).astype(jnp.bfloat16)
        for c in range(2):
            for t in range(3):
                at = (c * 3 + t) * TILE
                mb[c, :, t * 48 + g * 16 : t * 48 + g * 16 + 16, :] = term[
                    :, at : at + TILE
                ].reshape(chips, 16, TILE)
        d_key = jnp.where(diag, dot(ds_s[g], q[:, cols]), 0.0) * scale
        d_key = d_key.reshape(chips, 2, 8, 256)
        d_key = d_key[:, 0] + d_key[:, 1]
        d_key = d_key + pltpu.roll(d_key, 4, 1)
        key_tiles += [d_key[:, :, :TILE], d_key[:, :, TILE:]]
    low = lax.broadcasted_iota(jnp.int32, (chips, 8, TILE), 1) < 4
    for c in range(2):
        a, b, e = key_tiles[3 * c : 3 * c + 3]
        mb[c, :, 144:160, :] = jnp.concatenate(
            [jnp.where(low, a, b), jnp.where(low, e, 0.0)], axis=1
        ).astype(jnp.bfloat16)

    parts = (slice(0, 80), slice(80, 160))
    swaps = []
    for p, rs in enumerate(parts):
        copy = remote(
            mb.at[other, :, rs], pair.at[:, rs], pair_sem.at[0, p], pair_sem.at[1, p], sibling
        )
        copy.start()
        swaps.append(copy)
    store(kbd, kbd_hbm, out_sem.at[0])
    store(vbd, vbd_hbm, out_sem.at[1])
    store(ds_s, ds_hbm, out_sem.at[2])
    order = list(range(1, zs)) + [0]
    x_sent, z_sent, agz_out, agx_out, fw_out = [], [], [], [], []

    def summed(n, rs):
        return mb[core, n, rs].astype(jnp.float32) + pair[n, rs].astype(jnp.float32)

    for p, rs in enumerate(parts):
        swaps[p].wait_recv()
        for o in order:
            x_out[o, rs] = summed((1 - x) * zs + along(o)[0], rs).astype(jnp.bfloat16)
            copy = remote(
                x_out.at[o, rs], x_in.at[o, rs], x_send.at[p, o], x_recv.at[p, o], across
            )
            copy.start()
            x_sent.append(copy)
    for p, rs in enumerate(parts):
        for i, o in enumerate(order[:-1]):
            to, device = along(o)
            x_sent[p * zs + i].wait_recv()
            z_out[o - 1, rs] = (
                summed(x * zs + to, rs) + x_in[o, rs].astype(jnp.float32)
            ).astype(jnp.bfloat16)
            copy = remote(
                z_out.at[o - 1, rs], z_in.at[o - 1, rs], z_send.at[p, o - 1],
                z_recv.at[p, o - 1], device,
            )
            copy.start()
            z_sent.append(copy)

    def rows_of(p):
        return slice(0, 80) if p == 0 else slice(80, 144)

    def to_across(p, o):
        n = x * zs + along(zs - o)[0]
        at = ag.at[core, n, rows_of(p)]
        copy = remote(at, at, agx_send.at[p, o], agx_recv.at[p, o], across)
        copy.start()
        agx_out.append(copy)

    def piece(i):
        return (x if i < zs else 1 - x) * zs + along(zs - i % zs)[0]

    def to_sibling(p, i):
        n = piece(i)
        at = ag.at[core, n, rows_of(p)]
        copy = remote(at, at, fw_send.at[p, i], fw_recv.at[p, i], sibling)
        copy.start()
        fw_out.append(copy)

    def arrived(p, i):
        n = piece(i)
        at = ag.at[other, n, rows_of(p)]
        remote(at, at, fw_send.at[p, i], fw_recv.at[p, i], sibling).wait_recv()

    for p, rs in enumerate(parts):
        x_sent[p * zs + zs - 1].wait_recv()
        mine = summed(me, rs) + x_in[0, rs].astype(jnp.float32)
        for o in range(1, zs):
            z_sent[p * (zs - 1) + o - 1].wait_recv()
            mine = mine + z_in[o - 1, rs].astype(jnp.float32)
        if p == 0:
            ag[core, me, :80] = mine.astype(jnp.bfloat16)
        else:
            ag[core, me, 80:144] = mine[:64].astype(jnp.bfloat16)
            dk[core] = mine[64:]
        at = ag.at[core, me, rows_of(p)]
        for o in range(1, zs):
            copy = remote(at, at, agz_send.at[p, o - 1], agz_recv.at[p, o - 1], along(o)[1])
            copy.start()
            agz_out.append(copy)
        to_across(p, 0)
        to_sibling(p, 0)
    dk_copy = remote(dk.at[core], dk.at[core], dk_sem.at[0], dk_sem.at[1], sibling)
    dk_copy.start()
    for p in range(2):
        for o in range(1, zs):
            at = ag.at[core, piece(o), rows_of(p)]
            remote(
                at, at, agz_send.at[p, o - 1], agz_recv.at[p, o - 1], along(o)[1]
            ).wait_recv()
            to_across(p, o)
            to_sibling(p, o)

    def from_across(p, o):
        at = ag.at[core, piece(zs + o), rows_of(p)]
        remote(at, at, agx_send.at[p, o], agx_recv.at[p, o], across).wait_recv()
        to_sibling(p, zs + o)

    for p in range(2):
        for o in range(zs):
            from_across(p, o)

    remote(dk.at[other], dk.at[other], dk_sem.at[0], dk_sem.at[1], sibling).wait_recv()
    for c in range(2):
        for t in range(3):
            at = (c * 3 + t) * TILE
            gkv[:, at : at + TILE] = dk[c, t * 4 : t * 4 + 4, :]
    arrived(0, 0)
    arrived(1, 0)
    for g in range(groups):
        m_own = jnp.concatenate(
            [ag[c, me, t * 48 + g * 16 : t * 48 + g * 16 + 16, :] for c in range(2) for t in range(3)],
            axis=1,
        )
        r = jnp.where(diag[:16], dot(m_own, w[g * 256 : g * 256 + 256, :], NT), 0.0)
        r = r[:8] + r[8:]
        r = r + pltpu.roll(r, 4, 0)
        gkv[:, D + g * 256 : D + g * 256 + 256] = r[:4]
    store(gkv, gkv_hbm.at[0], out_sem.at[3])

    for p in range(2):
        for i in range(1, 2 * zs):
            arrived(p, i)
    store(ag, ag_hbm, out_sem.at[4])
    for copy in kv_out + swaps + x_sent + z_sent + agz_out + agx_out + fw_out + [dk_copy]:
        copy.wait_send()
    for copy in stores:
        copy.wait()


def last_kernel(
    ag_hbm, gkv_hbm, kbd_hbm, vbd_hbm, ds_hbm, gq_out, gkv_out, gw_out,
    ag, kbd, vbd, ds_s, gq, gw, in_sem, out_sem,
):
    scale = HEAD_DIM ** (-0.5)
    krows = kbd.shape[1]
    groups = HEADS // GROUP
    loads = [
        pltpu.make_async_copy(a, b, in_sem.at[i])
        for i, (a, b) in enumerate(((ds_hbm, ds_s), (kbd_hbm, kbd), (vbd_hbm, vbd), (ag_hbm, ag)))
    ]
    for load in loads:
        load.start()
    stores = [pltpu.make_async_copy(gkv_hbm, gkv_out, out_sem.at[0])]
    stores[0].start()
    loads[0].wait()
    loads[1].wait()
    for g in range(groups):
        cols = slice(g * 256, g * 256 + 256)
        gq[:, cols] = (dot(ds_s[g], kbd[g], TN) * scale).astype(jnp.bfloat16)
    stores.append(pltpu.make_async_copy(gq, gq_out, out_sem.at[1]))
    stores[1].start()
    loads[2].wait()
    loads[3].wait()
    for g in range(groups):
        m_g = jnp.concatenate(
            [
                ag[c, :, t * 48 + g * 16 : t * 48 + g * 16 + 16, :].reshape(krows, TILE)
                for c in range(2)
                for t in range(3)
            ],
            axis=1,
        )
        part = slice(g * 256, g * 256 + 256)
        gw[part, :] = dot(vbd[g], m_g, TN)
        stores.append(pltpu.make_async_copy(gw.at[part], gw_out.at[part], out_sem.at[2 + g]))
        stores[-1].start()
    for copy in stores:
        copy.wait()


def fused(xs, zs, query_heads, d_out, anchor_kv, point_counts, slot_car, out_weight):
    chips = xs * zs
    rows = query_heads.shape[0]
    bf, f32 = jnp.bfloat16, jnp.float32
    dma = lambda *n: pltpu.SemaphoreType.DMA(n)
    hbm = pl.BlockSpec(memory_space=pltpu.HBM)
    vmem = pl.BlockSpec(memory_space=pltpu.VMEM)
    limit = 60 * 1024 * 1024
    half_shape = (chips, 160, TILE)
    kd_shape = (3, chips * 16, 256)
    ds_shape = (3, chips * 16, rows)
    ag_shape = (2, chips, 144, TILE)
    mids = pl.pallas_call(
        functools.partial(fused_kernel, xs, zs),
        out_shape=(
            jax.ShapeDtypeStruct(ag_shape, bf),
            jax.ShapeDtypeStruct(anchor_kv.shape, f32),
            jax.ShapeDtypeStruct(kd_shape, bf),
            jax.ShapeDtypeStruct(kd_shape, bf),
            jax.ShapeDtypeStruct(ds_shape, bf),
        ),
        in_specs=[hbm, hbm, vmem, hbm, hbm, hbm],
        out_specs=(hbm,) * 5,
        scratch_shapes=[
            pltpu.SMEM(point_counts.shape, jnp.int32),
            pltpu.SMEM(slot_car.shape, jnp.int32),
            pltpu.VMEM((rows, D), bf),
            pltpu.VMEM((rows, D), bf),
            pltpu.VMEM((D, D), bf),
            pltpu.VMEM((48, TILE), f32),
            pltpu.VMEM((chips, 48, TILE), bf),
            pltpu.VMEM((rows, D), bf),
            pltpu.VMEM(kd_shape, bf),
            pltpu.VMEM(kd_shape, bf),
            pltpu.VMEM((chips * 16, rows), bf),
            pltpu.VMEM(ds_shape, bf),
            pltpu.VMEM((2,) + half_shape, bf),
            pltpu.VMEM(half_shape, bf),
            pltpu.VMEM((zs, 160, TILE), bf),
            pltpu.VMEM((zs, 160, TILE), bf),
            pltpu.VMEM((zs - 1, 160, TILE), bf),
            pltpu.VMEM((zs - 1, 160, TILE), bf),
            pltpu.VMEM(ag_shape, bf),
            pltpu.VMEM((2, 16, TILE), f32),
            pltpu.VMEM(anchor_kv.shape[1:], f32),
            dma(5),
            dma(chips - 1),
            dma(chips - 1),
            dma(2, 2),
            dma(2, zs),
            dma(2, zs),
            dma(2, zs - 1),
            dma(2, zs - 1),
            dma(2, zs - 1),
            dma(2, zs - 1),
            dma(2, zs),
            dma(2, zs),
            dma(2, chips),
            dma(2, chips),
            dma(2),
            dma(5),
        ],
        compiler_params=pltpu.CompilerParams(
            collective_id=0, has_side_effects=True, vmem_limit_bytes=limit
        ),
        cost_estimate=pl.CostEstimate(
            flops=2 * rows * D * D * 2, bytes_accessed=5 * 1024 * 1024, transcendentals=rows * 96
        ),
    )(point_counts, slot_car, anchor_kv, query_heads, d_out, out_weight)
    return pl.pallas_call(
        last_kernel,
        out_shape=(
            jax.ShapeDtypeStruct((rows, D), bf),
            jax.ShapeDtypeStruct(anchor_kv.shape, f32),
            jax.ShapeDtypeStruct((D, D), f32),
        ),
        in_specs=[hbm] * 5,
        out_specs=(hbm,) * 3,
        scratch_shapes=[
            pltpu.VMEM(ag_shape, bf),
            pltpu.VMEM(kd_shape, bf),
            pltpu.VMEM(kd_shape, bf),
            pltpu.VMEM(ds_shape, bf),
            pltpu.VMEM((rows, D), bf),
            pltpu.VMEM((D, D), f32),
            dma(4),
            dma(5),
        ],
        compiler_params=pltpu.CompilerParams(vmem_limit_bytes=limit),
        cost_estimate=pl.CostEstimate(
            flops=2 * rows * D * D, bytes_accessed=5 * 1024 * 1024, transcendentals=0
        ),
    )(*mids)


def choose(mesh):
    xs, zs, cores = mesh.shape["query"], mesh.shape["car"], mesh.shape["replica"]

    def run(query_heads, d_out, anchor_kv, point_counts, slot_car, out_weight):
        args = (query_heads, d_out, anchor_kv, point_counts, slot_car, out_weight)
        few = xs * zs == 8 and cores == 2 and anchor_kv.shape[:2] == (1, 4)
        if few and query_heads.shape[0] % TILE == 0:
            return fused(xs, zs, *args)
        return body(*args)

    return run


def solution(mesh):
    in_specs = (
        P(("groups", "query", "car", "replica"), None),
        P(("groups", "query", "car", "replica"), None),
        P(("groups", "car"), "query", None),
        P(("groups", "query", "car", "replica"), None),
        P("groups"),
        P(),
    )
    out_specs = (
        P(("groups", "query", "car", "replica"), None),
        P(("groups", "car"), "query", None),
        P("groups", None),
    )
    return jax.shard_map(choose(mesh), mesh=mesh, in_specs=in_specs, out_specs=out_specs, check_vma=False)
```

```python
import functools
import math

import jax
import jax.numpy as jnp
from jax import lax
from jax.experimental import pallas as pl
from jax.experimental.pallas import tpu as pltpu
from jax.sharding import PartitionSpec as P

D = 768
HEADS = 12
HEAD_DIM = 64


def head_view(values):
    return values.reshape(values.shape[0], HEADS, HEAD_DIM)


def car_lookup(start, count, anchors_each, owners, slot_car):
    rows = start + jnp.arange(count, dtype=jnp.int32)
    slots = rows // anchors_each % owners
    table = slots[:, None] == jnp.arange(slot_car.shape[0], dtype=jnp.int32)[None, :]
    return jnp.sum(jnp.where(table, slot_car[None, :], 0), axis=1)


def body(query_heads, d_out, anchor_kv, point_counts, slot_car, out_weight):
    scale = HEAD_DIM ** (-0.5)
    owners = lax.axis_size("car")
    anchors_each = anchor_kv.shape[1]
    rows_here = query_heads.shape[0]
    ends = jnp.cumsum(point_counts[0])
    local = jnp.arange(rows_here, dtype=jnp.int32)
    point_car = jnp.sum((local[:, None] >= ends[None, :]).astype(jnp.int32), axis=1)
    panel = anchor_kv[0]
    queries = head_view(query_heads)

    def allowed_for(start, count):
        cars = car_lookup(start, count, anchors_each, owners, slot_car)
        return (point_car[:, None] == cars[None, :])[:, None, :]

    def forward_step(carry, piece, start):
        best, total, accum = carry
        count = piece.shape[0]
        keys = head_view(piece[:, :D])
        values = head_view(piece[:, D:])
        allowed = allowed_for(start, count)
        scores = (
            jnp.einsum("qhe,khe->qhk", queries, keys, preferred_element_type=jnp.float32) * scale
        )
        peak = jnp.max(jnp.where(allowed, scores, -1e30), axis=2)
        new_best = jnp.maximum(best, peak)
        weights = jnp.where(allowed, jnp.exp(scores - new_best[:, :, None]), 0.0)
        fade = jnp.exp(best - new_best)
        total = total * fade + jnp.sum(weights, axis=2)
        accum = accum * fade[:, :, None] + jnp.einsum(
            "qhk,khe->qhe", weights.astype(jnp.bfloat16), values, preferred_element_type=jnp.float32
        )
        return (new_best, total, accum)

    init = (
        jnp.full((rows_here, HEADS), -1e30, jnp.float32),
        jnp.zeros((rows_here, HEADS), jnp.float32),
        jnp.zeros((rows_here, HEADS, HEAD_DIM), jnp.float32),
    )
    kv_all = lax.all_gather(panel, ("query", "car"), axis=0, tiled=True)
    key_rows = kv_all.shape[0]
    block = math.gcd(key_rows, 128)
    blocks = kv_all.reshape(key_rows // block, block, 2 * D)

    def scan_forward(carry, inputs):
        piece, number = inputs
        return (forward_step(carry, piece, number * block), None)

    (best, total, accum), _ = lax.scan(
        scan_forward, init, (blocks, jnp.arange(key_rows // block, dtype=jnp.int32))
    )
    numbers = jnp.arange(key_rows // block, dtype=jnp.int32)
    attended = (accum / total[:, :, None]).reshape(rows_here, D).astype(jnp.bfloat16)
    d_att = lax.dot_general(
        d_out, out_weight, (((1,), (1,)), ((), ())), preferred_element_type=jnp.float32
    ).astype(jnp.bfloat16)
    weight_term = lax.dot_general(
        attended, d_out, (((0,), (0,)), ((), ())), preferred_element_type=jnp.float32
    )
    weight_grad = lax.psum(weight_term, ("query", "car", "replica"))
    d_heads = head_view(d_att)
    delta = jnp.sum(d_heads.astype(jnp.float32) * head_view(attended).astype(jnp.float32), axis=2)

    def backward_step(d_query, inputs):
        piece, number = inputs
        keys = head_view(piece[:, :D])
        values = head_view(piece[:, D:])
        allowed = allowed_for(number * block, block)
        scores = (
            jnp.einsum("qhe,khe->qhk", queries, keys, preferred_element_type=jnp.float32) * scale
        )
        prob = jnp.where(allowed, jnp.exp(scores - best[:, :, None]), 0.0) / total[:, :, None]
        d_prob = jnp.einsum("qhe,khe->qhk", d_heads, values, preferred_element_type=jnp.float32)
        d_score = (prob * (d_prob - delta[:, :, None])).astype(jnp.bfloat16)
        d_query = d_query + jnp.einsum(
            "qhk,khe->qhe", d_score, keys, preferred_element_type=jnp.float32
        )
        d_key = (
            jnp.einsum("qhk,qhe->khe", d_score, queries, preferred_element_type=jnp.float32) * scale
        )
        d_value = jnp.einsum(
            "qhk,qhe->khe", prob.astype(jnp.bfloat16), d_heads, preferred_element_type=jnp.float32
        )
        return (
            d_query,
            jnp.concatenate([d_key.reshape(block, D), d_value.reshape(block, D)], axis=1),
        )

    d_query, stacked = lax.scan(
        backward_step, jnp.zeros((rows_here, HEADS, HEAD_DIM), jnp.float32), (blocks, numbers)
    )
    kv_term = stacked.reshape(key_rows, 2 * D)
    kv_part = lax.psum_scatter(kv_term, ("query", "car"), scatter_dimension=0, tiled=True)
    kv_mine = lax.psum(kv_part, "replica")
    grad_queries = (d_query * scale).reshape(rows_here, D).astype(jnp.bfloat16)
    return (grad_queries, kv_mine.reshape(1, anchors_each, 2 * D), weight_grad)


TILE = 128
GROUP = 4
NT = (((1,), (1,)), ((), ()))
TN = (((0,), (0,)), ((), ()))


def dot(a, b, dims=(((1,), (0,)), ((), ()))):
    return lax.dot_general(a, b, dims, preferred_element_type=jnp.float32)


def fused_kernel(
    xs, zs, counts_hbm, slots_hbm, kv, q_hbm, do_hbm, w_hbm, ag_hbm, gkv_hbm, kbd_hbm, vbd_hbm, ds_hbm,
    counts, slots, q, do, w, pack, kvall, da, kbd, vbd, prob_s, ds_s, mb, pair, x_out, x_in, z_out,
    z_in, ag, dk, gkv, in_sem, kv_send, kv_recv, pair_sem, x_send, x_recv, z_send, z_recv, agz_send,
    agz_recv, agx_send, agx_recv, fw_send, fw_recv, dk_sem, out_sem,
):
    scale = HEAD_DIM ** (-0.5)
    chips = xs * zs
    groups = HEADS // GROUP
    rows = q.shape[0]
    grp, x, z, core = (lax.axis_index(a) for a in ("groups", "query", "car", "replica"))
    me = x * zs + z
    other = 1 - core
    sibling = (grp, x, z, other)
    across = (grp, 1 - x, z, core)
    stores = []

    def store(src, dst, sem):
        copy = pltpu.make_async_copy(src, dst, sem)
        copy.start()
        stores.append(copy)

    def along(offset):
        to = line[offset % zs]
        return to, (grp, x, to, core)

    line = [z] + [lax.rem(z + offset, zs) for offset in range(1, zs)]

    def chip(offset):
        to_x = x if offset % chips < zs else 1 - x
        to_z = line[offset % zs]
        return to_x * zs + to_z, (grp, to_x, to_z, core)

    def source(offset):
        to_x = x if offset < zs else 1 - x
        return to_x * zs + line[(zs - offset % zs) % zs]

    def remote(src, dst, send, recv, device):
        return pltpu.make_async_remote_copy(
            src_ref=src, dst_ref=dst, send_sem=send, recv_sem=recv, device_id=device,
            device_id_type=pl.DeviceIdType.MESH,
        )

    loads = [
        pltpu.make_async_copy(a, b, in_sem.at[i])
        for i, (a, b) in enumerate(((do_hbm, do), (w_hbm, w), (q_hbm, q), (counts_hbm, counts), (slots_hbm, slots)))
    ]

    barrier = pltpu.get_barrier_semaphore()
    for offset in range(1, chips):
        pl.semaphore_signal(
            barrier, inc=1, device_id=chip(offset)[1], device_id_type=pl.DeviceIdType.MESH
        )
    pl.semaphore_signal(barrier, inc=1, device_id=sibling, device_id_type=pl.DeviceIdType.MESH)

    for load in loads:
        load.start()

    own_kv = kv[0].astype(jnp.float32)
    for h in range(HEADS):
        pack[h * 4 : h * 4 + 4, :HEAD_DIM] = own_kv[:, h * HEAD_DIM : (h + 1) * HEAD_DIM]
        pack[h * 4 : h * 4 + 4, HEAD_DIM:] = own_kv[:, D + h * HEAD_DIM : D + (h + 1) * HEAD_DIM]
    kvall[me] = pack[...].astype(jnp.bfloat16)

    pl.semaphore_wait(barrier, chips)
    kv_out = []
    for offset in range(1, chips):
        n, device = chip(offset)
        copy = remote(
            kvall.at[me], kvall.at[me], kv_send.at[offset - 1], kv_recv.at[offset - 1], device
        )
        copy.start()
        kv_out.append(copy)

    loads[0].wait()
    loads[1].wait()
    for g in range(groups):
        cols = slice(g * 256, g * 256 + 256)
        da[:, cols] = dot(do[...], w[cols, :], NT).astype(jnp.bfloat16)
    for load in loads[2:]:
        load.wait()

    lane = lax.broadcasted_iota(jnp.int32, (8, rows), 1)
    sub = lax.broadcasted_iota(jnp.int32, (8, rows), 0)
    masks = []
    for s in range(zs):
        car = slots[s]
        first = jnp.int32(0)
        size = jnp.int32(0)
        for c in range(counts.shape[1]):
            first = first + jnp.where(c < car, counts[0, c], 0)
            size = size + jnp.where(c == car, counts[0, c], 0)
        masks.append((lane >= first) & (lane < first + size))

    def swap(v, s):
        return jnp.where((sub & s) == 0, pltpu.roll(v, 8 - s, 0), pltpu.roll(v, s, 0))

    def over_four(v, op):
        v = op(v, swap(v, 1))
        return op(v, swap(v, 2))

    def pick(full, xi, hp):
        part = [full[(xi * zs + s) * 16 + hp * 8 : (xi * zs + s) * 16 + hp * 8 + 8, :] for s in range(zs)]
        out = part[0]
        for s in range(1, zs):
            out = jnp.where(masks[s], part[s], out)
        return out

    for offset in range(1, chips):
        n, device = source(offset), across
        remote(
            kvall.at[n], kvall.at[n], kv_send.at[offset - 1], kv_recv.at[offset - 1], device
        ).wait_recv()

    krows = chips * 16
    diag_row = lax.broadcasted_iota(jnp.int32, (krows, 256), 0) // 4 % GROUP
    diag = diag_row == lax.broadcasted_iota(jnp.int32, (krows, 256), 1) // HEAD_DIM
    half = lax.broadcasted_iota(jnp.int32, (krows, TILE), 1) < HEAD_DIM
    key_tiles = []
    for g in range(groups):
        cols = slice(g * 256, g * 256 + 256)
        both = kvall[:, g * 16 : g * 16 + 16, :].reshape(krows, TILE).astype(jnp.float32)
        turned = pltpu.roll(both, HEAD_DIM, 1)
        keys2 = jnp.where(half, both, turned)
        vals2 = jnp.where(half, turned, both)
        kd = jnp.where(diag, jnp.concatenate([keys2, keys2], axis=1), 0.0).astype(jnp.bfloat16)
        vd = jnp.where(diag, jnp.concatenate([vals2, vals2], axis=1), 0.0).astype(jnp.bfloat16)
        kbd[g] = kd
        vbd[g] = vd
        scores = dot(kd, q[:, cols], NT)
        d_prob = dot(vd, da[:, cols], NT)
        probs = [[None, None] for _ in range(xs)]
        dss = [[None, None] for _ in range(xs)]
        for hp in range(2):
            sc = [pick(scores, xi, hp) * scale for xi in range(xs)]
            dp = [pick(d_prob, xi, hp) for xi in range(xs)]
            best = over_four(functools.reduce(jnp.maximum, sc), jnp.maximum)
            wt = [jnp.exp(v - best) for v in sc]
            total = over_four(functools.reduce(jnp.add, wt), jnp.add)
            inv = 1.0 / total
            pr = [v * inv for v in wt]
            delta = over_four(functools.reduce(jnp.add, [a * b for a, b in zip(pr, dp)]), jnp.add)
            for xi in range(xs):
                probs[xi][hp] = pr[xi]
                dss[xi][hp] = pr[xi] * (dp[xi] - delta)
        for xi in range(xs):
            for s in range(zs):
                at = slice((xi * zs + s) * 16, (xi * zs + s) * 16 + 16)
                mask = jnp.concatenate([masks[s], masks[s]], axis=0)
                prob_s[at, :] = jnp.where(mask, jnp.concatenate(probs[xi], axis=0), 0.0).astype(
                    jnp.bfloat16
                )
                ds_s[g, at, :] = jnp.where(mask, jnp.concatenate(dss[xi], axis=0), 0.0).astype(
                    jnp.bfloat16
                )
        term = dot(prob_s[...], do[...]).astype(jnp.bfloat16)
        for c in range(2):
            for t in range(3):
                at = (c * 3 + t) * TILE
                mb[c, :, t * 48 + g * 16 : t * 48 + g * 16 + 16, :] = term[
                    :, at : at + TILE
                ].reshape(chips, 16, TILE)
        d_key = jnp.where(diag, dot(ds_s[g], q[:, cols]), 0.0) * scale
        d_key = d_key.reshape(chips, 2, 8, 256)
        d_key = d_key[:, 0] + d_key[:, 1]
        d_key = d_key + pltpu.roll(d_key, 4, 1)
        key_tiles += [d_key[:, :, :TILE], d_key[:, :, TILE:]]
    low = lax.broadcasted_iota(jnp.int32, (chips, 8, TILE), 1) < 4
    for c in range(2):
        a, b, e = key_tiles[3 * c : 3 * c + 3]
        mb[c, :, 144:160, :] = jnp.concatenate(
            [jnp.where(low, a, b), jnp.where(low, e, 0.0)], axis=1
        ).astype(jnp.bfloat16)

    parts = (slice(0, 80), slice(80, 160))
    swaps = []
    for p, rs in enumerate(parts):
        copy = remote(
            mb.at[other, :, rs], pair.at[:, rs], pair_sem.at[0, p], pair_sem.at[1, p], sibling
        )
        copy.start()
        swaps.append(copy)
    store(kbd, kbd_hbm, out_sem.at[0])
    store(vbd, vbd_hbm, out_sem.at[1])
    store(ds_s, ds_hbm, out_sem.at[2])
    order = list(range(1, zs)) + [0]
    x_sent, z_sent, agz_out, agx_out, fw_out = [], [], [], [], []

    def summed(n, rs):
        return mb[core, n, rs].astype(jnp.float32) + pair[n, rs].astype(jnp.float32)

    for p, rs in enumerate(parts):
        swaps[p].wait_recv()
        for o in order:
            x_out[o, rs] = summed((1 - x) * zs + along(o)[0], rs).astype(jnp.bfloat16)
            copy = remote(
                x_out.at[o, rs], x_in.at[o, rs], x_send.at[p, o], x_recv.at[p, o], across
            )
            copy.start()
            x_sent.append(copy)
    for p, rs in enumerate(parts):
        for i, o in enumerate(order[:-1]):
            to, device = along(o)
            x_sent[p * zs + i].wait_recv()
            z_out[o - 1, rs] = (
                summed(x * zs + to, rs) + x_in[o, rs].astype(jnp.float32)
            ).astype(jnp.bfloat16)
            copy = remote(
                z_out.at[o - 1, rs], z_in.at[o - 1, rs], z_send.at[p, o - 1],
                z_recv.at[p, o - 1], device,
            )
            copy.start()
            z_sent.append(copy)

    def rows_of(p):
        return slice(0, 80) if p == 0 else slice(80, 144)

    def to_across(p, o):
        n = x * zs + along(zs - o)[0]
        at = ag.at[core, n, rows_of(p)]
        copy = remote(at, at, agx_send.at[p, o], agx_recv.at[p, o], across)
        copy.start()
        agx_out.append(copy)

    def piece(i):
        return (x if i < zs else 1 - x) * zs + along(zs - i % zs)[0]

    def to_sibling(p, i):
        n = piece(i)
        at = ag.at[core, n, rows_of(p)]
        copy = remote(at, at, fw_send.at[p, i], fw_recv.at[p, i], sibling)
        copy.start()
        fw_out.append(copy)

    def arrived(p, i):
        n = piece(i)
        at = ag.at[other, n, rows_of(p)]
        remote(at, at, fw_send.at[p, i], fw_recv.at[p, i], sibling).wait_recv()

    for p, rs in enumerate(parts):
        x_sent[p * zs + zs - 1].wait_recv()
        mine = summed(me, rs) + x_in[0, rs].astype(jnp.float32)
        for o in range(1, zs):
            z_sent[p * (zs - 1) + o - 1].wait_recv()
            mine = mine + z_in[o - 1, rs].astype(jnp.float32)
        if p == 0:
            ag[core, me, :80] = mine.astype(jnp.bfloat16)
        else:
            ag[core, me, 80:144] = mine[:64].astype(jnp.bfloat16)
            dk[core] = mine[64:]
        at = ag.at[core, me, rows_of(p)]
        for o in range(1, zs):
            copy = remote(at, at, agz_send.at[p, o - 1], agz_recv.at[p, o - 1], along(o)[1])
            copy.start()
            agz_out.append(copy)
        to_across(p, 0)
        to_sibling(p, 0)
    dk_copy = remote(dk.at[core], dk.at[core], dk_sem.at[0], dk_sem.at[1], sibling)
    dk_copy.start()
    for p in range(2):
        for o in range(1, zs):
            at = ag.at[core, piece(o), rows_of(p)]
            remote(
                at, at, agz_send.at[p, o - 1], agz_recv.at[p, o - 1], along(o)[1]
            ).wait_recv()
            to_across(p, o)
            to_sibling(p, o)

    def from_across(p, o):
        at = ag.at[core, piece(zs + o), rows_of(p)]
        remote(at, at, agx_send.at[p, o], agx_recv.at[p, o], across).wait_recv()
        to_sibling(p, zs + o)

    for p in range(2):
        for o in range(zs):
            from_across(p, o)

    remote(dk.at[other], dk.at[other], dk_sem.at[0], dk_sem.at[1], sibling).wait_recv()
    for c in range(2):
        for t in range(3):
            at = (c * 3 + t) * TILE
            gkv[:, at : at + TILE] = dk[c, t * 4 : t * 4 + 4, :]
    arrived(0, 0)
    arrived(1, 0)
    for g in range(groups):
        m_own = jnp.concatenate(
            [ag[c, me, t * 48 + g * 16 : t * 48 + g * 16 + 16, :] for c in range(2) for t in range(3)],
            axis=1,
        )
        r = jnp.where(diag[:16], dot(m_own, w[g * 256 : g * 256 + 256, :], NT), 0.0)
        r = r[:8] + r[8:]
        r = r + pltpu.roll(r, 4, 0)
        gkv[:, D + g * 256 : D + g * 256 + 256] = r[:4]
    store(gkv, gkv_hbm.at[0], out_sem.at[3])

    for p in range(2):
        for i in range(1, 2 * zs):
            arrived(p, i)
    store(ag, ag_hbm, out_sem.at[4])
    for copy in kv_out + swaps + x_sent + z_sent + agz_out + agx_out + fw_out + [dk_copy]:
        copy.wait_send()
    for copy in stores:
        copy.wait()


def last_kernel(
    ag_hbm, gkv_hbm, kbd_hbm, vbd_hbm, ds_hbm, gq_out, gkv_out, gw_out,
    ag, kbd, vbd, ds_s, gq, gw, in_sem, out_sem,
):
    scale = HEAD_DIM ** (-0.5)
    krows = kbd.shape[1]
    groups = HEADS // GROUP
    loads = [
        pltpu.make_async_copy(a, b, in_sem.at[i])
        for i, (a, b) in enumerate(((ds_hbm, ds_s), (kbd_hbm, kbd), (vbd_hbm, vbd), (ag_hbm, ag)))
    ]
    for load in loads:
        load.start()
    stores = [pltpu.make_async_copy(gkv_hbm, gkv_out, out_sem.at[0])]
    stores[0].start()
    loads[0].wait()
    loads[1].wait()
    for g in range(groups):
        cols = slice(g * 256, g * 256 + 256)
        gq[:, cols] = (dot(ds_s[g], kbd[g], TN) * scale).astype(jnp.bfloat16)
    stores.append(pltpu.make_async_copy(gq, gq_out, out_sem.at[1]))
    stores[1].start()
    loads[2].wait()
    loads[3].wait()
    for g in range(groups):
        m_g = jnp.concatenate(
            [
                ag[c, :, t * 48 + g * 16 : t * 48 + g * 16 + 16, :].reshape(krows, TILE)
                for c in range(2)
                for t in range(3)
            ],
            axis=1,
        )
        part = slice(g * 256, g * 256 + 256)
        gw[part, :] = dot(vbd[g], m_g, TN)
        stores.append(pltpu.make_async_copy(gw.at[part], gw_out.at[part], out_sem.at[2 + g]))
        stores[-1].start()
    for copy in stores:
        copy.wait()


def fused(xs, zs, query_heads, d_out, anchor_kv, point_counts, slot_car, out_weight):
    chips = xs * zs
    rows = query_heads.shape[0]
    bf, f32 = jnp.bfloat16, jnp.float32
    dma = lambda *n: pltpu.SemaphoreType.DMA(n)
    hbm = pl.BlockSpec(memory_space=pltpu.HBM)
    vmem = pl.BlockSpec(memory_space=pltpu.VMEM)
    limit = 60 * 1024 * 1024
    half_shape = (chips, 160, TILE)
    kd_shape = (3, chips * 16, 256)
    ds_shape = (3, chips * 16, rows)
    ag_shape = (2, chips, 144, TILE)
    mids = pl.pallas_call(
        functools.partial(fused_kernel, xs, zs),
        out_shape=(
            jax.ShapeDtypeStruct(ag_shape, bf),
            jax.ShapeDtypeStruct(anchor_kv.shape, f32),
            jax.ShapeDtypeStruct(kd_shape, bf),
            jax.ShapeDtypeStruct(kd_shape, bf),
            jax.ShapeDtypeStruct(ds_shape, bf),
        ),
        in_specs=[hbm, hbm, vmem, hbm, hbm, hbm],
        out_specs=(hbm,) * 5,
        scratch_shapes=[
            pltpu.SMEM(point_counts.shape, jnp.int32),
            pltpu.SMEM(slot_car.shape, jnp.int32),
            pltpu.VMEM((rows, D), bf),
            pltpu.VMEM((rows, D), bf),
            pltpu.VMEM((D, D), bf),
            pltpu.VMEM((48, TILE), f32),
            pltpu.VMEM((chips, 48, TILE), bf),
            pltpu.VMEM((rows, D), bf),
            pltpu.VMEM(kd_shape, bf),
            pltpu.VMEM(kd_shape, bf),
            pltpu.VMEM((chips * 16, rows), bf),
            pltpu.VMEM(ds_shape, bf),
            pltpu.VMEM((2,) + half_shape, bf),
            pltpu.VMEM(half_shape, bf),
            pltpu.VMEM((zs, 160, TILE), bf),
            pltpu.VMEM((zs, 160, TILE), bf),
            pltpu.VMEM((zs - 1, 160, TILE), bf),
            pltpu.VMEM((zs - 1, 160, TILE), bf),
            pltpu.VMEM(ag_shape, bf),
            pltpu.VMEM((2, 16, TILE), f32),
            pltpu.VMEM(anchor_kv.shape[1:], f32),
            dma(5),
            dma(chips - 1),
            dma(chips - 1),
            dma(2, 2),
            dma(2, zs),
            dma(2, zs),
            dma(2, zs - 1),
            dma(2, zs - 1),
            dma(2, zs - 1),
            dma(2, zs - 1),
            dma(2, zs),
            dma(2, zs),
            dma(2, chips),
            dma(2, chips),
            dma(2),
            dma(5),
        ],
        compiler_params=pltpu.CompilerParams(
            collective_id=0, has_side_effects=True, vmem_limit_bytes=limit
        ),
        cost_estimate=pl.CostEstimate(
            flops=2 * rows * D * D * 2, bytes_accessed=5 * 1024 * 1024, transcendentals=rows * 96
        ),
    )(point_counts, slot_car, anchor_kv, query_heads, d_out, out_weight)
    return pl.pallas_call(
        last_kernel,
        out_shape=(
            jax.ShapeDtypeStruct((rows, D), bf),
            jax.ShapeDtypeStruct(anchor_kv.shape, f32),
            jax.ShapeDtypeStruct((D, D), f32),
        ),
        in_specs=[hbm] * 5,
        out_specs=(hbm,) * 3,
        scratch_shapes=[
            pltpu.VMEM(ag_shape, bf),
            pltpu.VMEM(kd_shape, bf),
            pltpu.VMEM(kd_shape, bf),
            pltpu.VMEM(ds_shape, bf),
            pltpu.VMEM((rows, D), bf),
            pltpu.VMEM((D, D), f32),
            dma(4),
            dma(5),
        ],
        compiler_params=pltpu.CompilerParams(vmem_limit_bytes=limit),
        cost_estimate=pl.CostEstimate(
            flops=2 * rows * D * D, bytes_accessed=5 * 1024 * 1024, transcendentals=0
        ),
    )(*mids)


def choose(mesh):
    xs, zs, cores = mesh.shape["query"], mesh.shape["car"], mesh.shape["replica"]

    def run(query_heads, d_out, anchor_kv, point_counts, slot_car, out_weight):
        args = (query_heads, d_out, anchor_kv, point_counts, slot_car, out_weight)
        few = xs * zs == 8 and cores == 2 and anchor_kv.shape[:2] == (1, 4)
        if few and query_heads.shape[0] % TILE == 0:
            return fused(xs, zs, *args)
        return body(*args)

    return run


def solution(mesh):
    in_specs = (
        P(("groups", "query", "car", "replica"), None),
        P(("groups", "query", "car", "replica"), None),
        P(("groups", "car"), "query", None),
        P(("groups", "query", "car", "replica"), None),
        P("groups"),
        P(),
    )
    out_specs = (
        P(("groups", "query", "car", "replica"), None),
        P(("groups", "car"), "query", None),
        P("groups", None),
    )
    return jax.shard_map(choose(mesh), mesh=mesh, in_specs=in_specs, out_specs=out_specs, check_vma=False)
```
